32 devices in a mesh: seq: 8 (over z, core), tensor: 4 (over y, x).
Axes of the slice: x: 2, y: 2, z: 4, core: 2. Of those that a mesh axis runs over, the one named last changes fastest.
Arguments:
- activations: bfloat16 [1024, 131072], P('tensor', 'seq'), may hold values from -24 to 24
- first_factor: bfloat16 [512, 512], replicated, may hold values from -0.25 to 0.25
- spectral: float32 [1024, 131072], P('tensor', 'seq'), may hold values from -4 to 4
- second_factor: float32 [256, 256], replicated, may hold values from -0.375 to 0.375
- gate_scale: float32 [1024], replicated, may hold values from -4 to 4
- gate_shift: float32 [1024], replicated, may hold values from -4 to 4
- expand_weight: bfloat16 [1024, 6144], P(None, ('seq', 'tensor')), may hold values from -0.1875 to 0.1875
- reduce_weight: bfloat16 [6144, 1024], P(('seq', 'tensor')), may hold values from -0.15625 to 0.15625
Outputs:
- layer_out: bfloat16 [1024, 131072], P('tensor', 'seq')
The draws below stay inside these ranges and needn't reach their ends.
All inputs are finite; a program needn't handle non-finite values.
Results may differ from the reference program's by a relative error of at most 0.0052.
Values may be sent and summed in bfloat16 or wider, within the bound.
No kernel may reach another device: no remote copies, remote signals or barrier semaphores. Data moves between devices by JAX's collectives and lax.ppermute only.
A program may use at most 192 MiB of HBM per device.

```python
import math
import jax
import jax.numpy as jnp
from jax import lax

A = 256
B = 512
C = 1024
H = 6144
TOKENS = 131072
DEVICES = 32


def draw_activations(key, part):
    key_chan, key_base, key_rows = jax.random.split(key, 3)
    channel_scale = jnp.exp(jax.random.uniform(key_chan, (C, 1), jnp.float32, math.log(0.3), math.log(3.0)))
    row_scale = jnp.exp(jax.random.uniform(key_rows, (1, A * B), jnp.float32, math.log(0.5), math.log(2.0)))
    base = jax.random.truncated_normal(key_base, -4.0, 4.0, (C, A * B), jnp.float32)
    return (base * channel_scale * row_scale).astype(jnp.bfloat16)


def strengthened(array, rng, source, target, parts, factor):
    owner, partner = [(jnp.arange(array.shape[axis_at]) // (array.shape[axis_at] // parts)).reshape([-1 if axis == axis_at else 1 for axis in range(array.ndim)]) for axis_at in (source, target)]
    chosen = jax.random.permutation(rng, parts)[partner]
    strong = (owner == chosen) | (owner == (partner + parts // 2) % parts)
    return jnp.where(strong, factor * array, array)


def block_levels(stream_key, shape, cuts, smallest, largest):
    def one(position, blocks):
        steps = jax.random.uniform(jax.random.fold_in(jax.random.fold_in(stream_key, 6), position), (blocks,), jnp.float32, smallest / len(cuts), largest / len(cuts))
        return jnp.repeat(jnp.exp(steps), shape[position] // blocks).reshape((-1,) + (1,) * (len(shape) - position - 1))

    factor_of = one(*cuts[0])
    for cut in cuts[1:]:
        factor_of = factor_of * one(*cut)
    return factor_of


def scatter_about(key, extent, spread, reach, pieces=(), kind=jnp.bfloat16):
    values = jax.random.normal(key, extent, jnp.float32) * spread
    if len(pieces) > 0:
        values = block_levels(key, extent, pieces, -0.22, 0.18) * values
    return jnp.clip(values, min=-reach, max=reach).astype(kind)


def noise_with(rng, dims, width, limit, pieces, heavy, dtype=jnp.bfloat16):
    values = width * jax.random.normal(rng, dims, jnp.float32)
    if pieces:
        values = values * block_levels(rng, dims, pieces, -0.22, 0.18)
    return jnp.clip(strengthened(values, jax.random.fold_in(rng, 3), *heavy), -limit, limit).astype(dtype)


def setup_inputs(seed: int = 0) -> dict:
    key_list = jax.random.split(jax.random.key(seed), 9)
    activations = draw_activations(jax.random.fold_in(key_list[8], 71), 0)
    first_factor = scatter_about(key_list[1], (B, B), B ** -0.5, 0.25)
    spectral = scatter_about(key_list[2], (C, TOKENS), 1.0, 4.0, ((0, 4), (1, 8)), jnp.float32)
    second_factor = scatter_about(key_list[3], (A, A), A ** -0.5, 0.375, (), jnp.float32)
    gate_scale = scatter_about(key_list[4], (C,), 1.0, 4.0, (), jnp.float32)
    gate_shift = scatter_about(key_list[5], (C,), 1.0, 4.0, (), jnp.float32)
    expand_weight = scatter_about(key_list[6], (C, H), C ** -0.5, 0.1875, ((1, 32),))
    reduce_weight = noise_with(key_list[7], (H, C), H ** -0.5, 0.15625, ((0, 32),), (0, 1, 32, 2.75))
    return {"activations": activations, "first_factor": first_factor, "spectral": spectral, "second_factor": second_factor, "gate_scale": gate_scale, "gate_shift": gate_shift, "expand_weight": expand_weight, "reduce_weight": reduce_weight}


epsilon = 1e-06

def reference(activations, first_factor, spectral, second_factor, gate_scale, gate_shift, expand_weight, reduce_weight):
    inputs = activations.astype(jnp.float32)
    blocks = inputs.reshape(C, A, B)
    first_pass = jnp.einsum('cai,ij->caj', blocks, first_factor.astype(jnp.float32))
    spectrum = first_pass * spectral.reshape(C, A, B)
    mixed = jnp.einsum('pa,caj->cpj', second_factor, spectrum, precision=lax.Precision.HIGHEST)
    gating = jax.nn.sigmoid(inputs * gate_scale[:, None] + gate_shift[:, None])
    residual_in = (inputs + gating * mixed.reshape(C, A * B)).astype(jnp.bfloat16)
    tile_width = A * B // DEVICES
    token_tiles = residual_in.reshape(C, DEVICES, tile_width).transpose(1, 0, 2)

    def apply_layer(columns):
        values = columns.astype(jnp.float32)
        scale = lax.rsqrt(lax.optimization_barrier(jnp.mean(values * values, axis=0, keepdims=True)) + epsilon)
        normed = (values * scale).astype(jnp.bfloat16)
        hidden = jax.nn.gelu(jnp.dot(expand_weight.T, normed, preferred_element_type=jnp.float32)).astype(jnp.bfloat16)
        mlp_out = jnp.dot(reduce_weight.T, hidden, preferred_element_type=jnp.float32)
        return (values + mlp_out).astype(jnp.bfloat16)
    results = lax.map(apply_layer, token_tiles)
    return results.transpose(1, 0, 2).reshape(C, A * B)
```

```python
import jax
import jax.numpy as jnp
from jax import lax
from jax.sharding import PartitionSpec as P

B = 512
COLUMNS = 128
epsilon = 1e-06


def normalize(block):
    values = block.astype(jnp.float32)
    scale = lax.rsqrt(jnp.mean(values * values, axis=0, keepdims=True) + epsilon)
    return (values * scale).astype(jnp.bfloat16)


def expand(normed, shard_rows):
    product = jnp.einsum("ch,cl->hl", shard_rows, normed, preferred_element_type=jnp.float32)
    return jax.nn.gelu(product).astype(jnp.bfloat16)


def on_device(
    activations,
    first_factor,
    spectral,
    second_factor,
    gate_scale,
    gate_shift,
    expand_weight,
    reduce_weight,
):
    channels = activations.shape[0]
    blocks = activations.shape[1] // B
    offset = lax.axis_index("tensor") * channels
    scale_here = lax.dynamic_slice_in_dim(gate_scale, offset, channels)[:, None, None]
    shift_here = lax.dynamic_slice_in_dim(gate_shift, offset, channels)[:, None, None]
    weight_in = lax.all_gather(expand_weight, ("seq", "tensor"), axis=1, tiled=True)
    weight_out = lax.all_gather(reduce_weight, ("seq", "tensor"), axis=0, tiled=True)
    act3 = activations.reshape(channels, blocks, B)
    spec3 = spectral.reshape(channels, blocks, B)
    high = lax.reduce_precision(second_factor, 8, 7)
    low = (second_factor - high).astype(jnp.bfloat16)
    high = high.astype(jnp.bfloat16)

    outs = []
    for start in range(0, B, COLUMNS):
        stop = start + COLUMNS
        first_pass = jnp.einsum(
            "cai,ij->caj", act3, first_factor[:, start:stop], preferred_element_type=jnp.float32
        )
        spectrum = (first_pass * spec3[:, :, start:stop]).astype(jnp.bfloat16)
        gathered = lax.all_to_all(spectrum, "seq", split_axis=0, concat_axis=1, tiled=True)
        mixed = jnp.einsum("pa,caj->cpj", high, gathered, preferred_element_type=jnp.float32)
        mixed += jnp.einsum("pa,caj->cpj", low, gathered, preferred_element_type=jnp.float32)
        returned = lax.all_to_all(
            mixed.astype(jnp.bfloat16), "seq", split_axis=1, concat_axis=0, tiled=True
        )
        inputs = act3[:, :, start:stop].astype(jnp.float32)
        gating = jax.nn.sigmoid(inputs * scale_here + shift_here)
        residual_in = (inputs + gating * returned.astype(jnp.float32)).astype(jnp.bfloat16)
        token_block = lax.all_to_all(residual_in, "tensor", split_axis=1, concat_axis=0, tiled=True)
        shape = token_block.shape
        token_block = token_block.reshape(shape[0], -1)
        hidden = expand(normalize(token_block), weight_in)
        summed = jnp.einsum("hc,hl->cl", weight_out, hidden, preferred_element_type=jnp.float32)
        combined = (token_block.astype(jnp.float32) + summed).astype(jnp.bfloat16).reshape(shape)
        outs.append(lax.all_to_all(combined, "tensor", split_axis=0, concat_axis=1, tiled=True))
    return jnp.concatenate(outs, axis=2).reshape(channels, -1)


def solution(mesh):
    return jax.shard_map(
        on_device,
        mesh=mesh,
        in_specs=(
            P("tensor", "seq"),
            P(),
            P("tensor", "seq"),
            P(),
            P(),
            P(),
            P(None, ("seq", "tensor")),
            P(("seq", "tensor"), None),
        ),
        out_specs=P("tensor", "seq"),
        check_vma=False,
    )
```

```python
import functools

import jax
import jax.numpy as jnp
from jax import lax
from jax.experimental import pallas as pl
from jax.experimental.pallas import tpu as pltpu
from jax.sharding import PartitionSpec as P

B = 512
J = 128
epsilon = 1e-06
f32 = jnp.float32
bf16 = jnp.bfloat16
ANY = pl.BlockSpec(memory_space=pl.ANY)


def params(mib):
    return pltpu.CompilerParams(vmem_limit_bytes=mib * 2**20)


def first_pass(k, activations, first_factor, spectral, ns, dep):
    c, tokens = activations.shape
    blocks = tokens // B
    step = min(4, blocks)
    per = B // J
    deps = [] if dep is None else [dep]

    def kernel(act, factor, *rest):
        specs, out = rest[:step], rest[-1]
        for q in range(step):
            product = jnp.dot(act[:, q * B : (q + 1) * B], factor[...], preferred_element_type=f32)
            value = (product * specs[q][...]).astype(bf16)
            out[:, q] = value.reshape(ns, c // ns, J)

    def spec_at(q):
        return pl.BlockSpec((c, J), lambda i: (0, (i * step + q) * per + k))

    return pl.pallas_call(
        kernel,
        grid=(blocks // step,),
        in_specs=[
            pl.BlockSpec((c, step * B), lambda i: (0, i)),
            pl.BlockSpec((B, J), lambda i: (0, k)),
        ]
        + [spec_at(q) for q in range(step)]
        + [ANY] * len(deps),
        out_specs=pl.BlockSpec((ns, step, c // ns, J), lambda i: (0, i, 0, 0)),
        out_shape=jax.ShapeDtypeStruct((ns, blocks, c // ns, J), bf16),
        compiler_params=params(32),
        cost_estimate=pl.CostEstimate(
            flops=4 * c * blocks * B * J,
            bytes_accessed=2 * c * tokens + 6 * c * blocks * J,
            transcendentals=0,
        ),
    )(activations, first_factor, *[spectral] * step, *deps)


def second_pass(gathered, second_factor, deps):
    a, c, _ = gathered.shape
    cb = min(16, c)

    def kernel(x_ref, s_ref, *rest):
        out, x_wide, y_wide = rest[-3:]
        x_wide[...] = x_ref[...].astype(f32).reshape(a * cb, J)
        factor = s_ref[...]
        high = factor.astype(bf16)
        low = (factor - high.astype(f32)).astype(bf16)
        for i in range(0, cb, 2):
            x = jnp.concatenate(
                [x_wide[pl.ds(i + n, a, stride=cb), :] for n in range(2)], axis=1
            ).astype(bf16)
            y = jnp.dot(high, x, preferred_element_type=f32)
            y += jnp.dot(low, x, preferred_element_type=f32)
            for n in range(2):
                y_wide[pl.ds(i + n, a, stride=cb), :] = y[:, n * J : (n + 1) * J]
        out[...] = y_wide[...].reshape(a, cb, J).astype(bf16)

    return pl.pallas_call(
        kernel,
        grid=(c // cb,),
        in_specs=[
            pl.BlockSpec((a, cb, J), lambda i: (0, i, 0)),
            pl.BlockSpec((a, a), lambda i: (0, 0)),
        ]
        + [ANY] * len(deps),
        out_specs=pl.BlockSpec((a, cb, J), lambda i: (0, i, 0)),
        out_shape=jax.ShapeDtypeStruct((a, c, J), bf16),
        scratch_shapes=[pltpu.VMEM((a * cb, J), f32), pltpu.VMEM((a * cb, J), f32)],
        compiler_params=params(32),
        cost_estimate=pl.CostEstimate(
            flops=8 * a * a * c * J, bytes_accessed=4 * a * c * J, transcendentals=0
        ),
    )(gathered, second_factor, *deps)


def gate(k, me, activations, returned, scale, shift, nt, deps):
    c, tokens = activations.shape
    ns, blocks, ci, _ = returned.shape
    mine = blocks // nt
    step = min(2, mine)
    steps = mine // step

    def kernel(me_ref, *rest):
        acts, rets = rest[:nt], rest[nt : 2 * nt]
        scale_ref, shift_ref = rest[2 * nt : 2 * nt + 2]
        outs = rest[-nt:]
        for s in range(nt):
            for q in range(step):
                x = acts[s][:, q * B + k * J : q * B + (k + 1) * J].astype(f32)
                mixed = rets[s][:, q].reshape(c, J).astype(f32)
                gating = jax.nn.sigmoid(x * scale_ref[...] + shift_ref[...])
                outs[s][:, q * J : (q + 1) * J] = (x + gating * mixed).astype(bf16)

    def act_at(s):
        return pl.BlockSpec((c, step * B), lambda i, me: (0, (me[0] ^ s) * steps + i))

    def ret_at(s):
        return pl.BlockSpec(
            (ns, step, ci, J), lambda i, me: (0, (me[0] ^ s) * steps + i, 0, 0)
        )

    column = pl.BlockSpec((c, 1), lambda i, me: (0, 0))
    return pl.pallas_call(
        kernel,
        grid_spec=pltpu.PrefetchScalarGridSpec(
            num_scalar_prefetch=1,
            grid=(steps,),
            in_specs=[act_at(s) for s in range(nt)]
            + [ret_at(s) for s in range(nt)]
            + [column, column]
            + [ANY] * len(deps),
            out_specs=[pl.BlockSpec((c, step * J), lambda i, me: (0, i))] * nt,
        ),
        out_shape=[jax.ShapeDtypeStruct((c, mine * J), bf16)] * nt,
        compiler_params=params(32),
        cost_estimate=pl.CostEstimate(
            flops=8 * c * blocks * J,
            bytes_accessed=2 * c * tokens + 4 * c * blocks * J,
            transcendentals=c * blocks * J,
        ),
    )(me, *[activations] * nt, *[returned] * nt, scale, shift, *deps)


def mlp(me, slots, weight_in, weight_out, deps):
    nt = len(slots)
    c, tokens = slots[0].shape
    hidden, full = weight_in.shape
    hb = hidden // 8
    tile = min(256, tokens)

    def kernel(me_ref, *rest):
        xs, (w1, w2) = rest[:nt], rest[nt : nt + 2]
        outs = rest[-nt - 2 : -2]
        normed, total = rest[-2:]
        step = pl.program_id(0)

        @pl.when(step == 0)
        def _():
            squares = jnp.zeros((1, tokens), f32)
            for s in range(nt):
                x = xs[s][...].astype(f32)
                squares += jnp.sum(x * x, axis=0, keepdims=True)
            scale = lax.rsqrt(squares / full + epsilon)
            for s in range(nt):
                at = pl.multiple_of((me_ref[0] ^ s) * c, c)
                normed[pl.ds(at, c), :] = (xs[s][...].astype(f32) * scale).astype(bf16)
            total[...] = jnp.zeros_like(total)

        for t in range(0, tokens, tile):
            x = jnp.dot(w1[...], normed[:, t : t + tile], preferred_element_type=f32)
            h = jax.nn.gelu(x).astype(bf16)
            total[:, t : t + tile] += jnp.dot(w2[...], h, preferred_element_type=f32)

        @pl.when(step == pl.num_programs(0) - 1)
        def _():
            for s in range(nt):
                at = pl.multiple_of((me_ref[0] ^ s) * c, c)
                outs[s][...] = (xs[s][...].astype(f32) + total[pl.ds(at, c), :]).astype(bf16)

    whole = pl.BlockSpec((c, tokens), lambda i, me: (0, 0))
    return pl.pallas_call(
        kernel,
        grid_spec=pltpu.PrefetchScalarGridSpec(
            num_scalar_prefetch=1,
            grid=(hidden // hb,),
            in_specs=[whole] * nt
            + [
                pl.BlockSpec((hb, full), lambda i, me: (i, 0)),
                pl.BlockSpec((full, hb), lambda i, me: (0, i)),
            ]
            + [ANY] * len(deps),
            out_specs=[whole] * nt,
            scratch_shapes=[pltpu.VMEM((full, tokens), bf16), pltpu.VMEM((full, tokens), f32)],
        ),
        out_shape=[jax.ShapeDtypeStruct((c, tokens), bf16)] * nt,
        compiler_params=params(40),
        cost_estimate=pl.CostEstimate(
            flops=4 * full * hidden * tokens,
            bytes_accessed=4 * full * hidden + 4 * full * tokens,
            transcendentals=hidden * tokens,
        ),
    )(me, *slots, weight_in, weight_out, *deps)


def place(k, me, slots, result, shape):
    nt = len(slots)
    c, tokens = slots[0].shape
    mine = tokens // J
    given = [] if result is None else [result]

    def kernel(me_ref, *rest):
        ys, out, sems = rest[:nt], rest[-2], rest[-1]
        copies = []
        for s in range(nt):
            for q in range(mine):
                at = pl.multiple_of(((me_ref[0] ^ s) * mine + q) * B + k * J, J)
                copies.append(
                    pltpu.make_async_copy(
                        ys[s].at[:, q * J : (q + 1) * J],
                        out.at[:, pl.ds(at, J)],
                        sems.at[s * mine + q],
                    )
                )
        for copy in copies:
            copy.start()
        for copy in copies:
            copy.wait()

    return pl.pallas_call(
        kernel,
        in_specs=[pl.BlockSpec(memory_space=pltpu.SMEM)] + [ANY] * (nt + len(given)),
        out_specs=ANY,
        out_shape=jax.ShapeDtypeStruct(shape, bf16),
        scratch_shapes=[pltpu.SemaphoreType.DMA((nt * mine,))],
        input_output_aliases={1 + nt: 0} if given else {},
        cost_estimate=pl.CostEstimate(
            flops=0, bytes_accessed=4 * c * tokens * nt, transcendentals=0
        ),
    )(me, *slots, *given)


def swap(slots):
    n = len(slots)
    return [slots[0]] + [
        lax.ppermute(slots[s], "tensor", [(i, i ^ s) for i in range(n)]) for s in range(1, n)
    ]


def on_device(
    ns,
    nt,
    activations,
    first_factor,
    spectral,
    second_factor,
    gate_scale,
    gate_shift,
    expand_weight,
    reduce_weight,
):
    c = activations.shape[0]
    full = expand_weight.shape[0]
    at = lax.axis_index("tensor")
    me = at.astype(jnp.int32).reshape(1)
    scale = lax.dynamic_slice_in_dim(gate_scale, at * c, c)[:, None]
    shift = lax.dynamic_slice_in_dim(gate_shift, at * c, c)[:, None]
    weight_in = lax.all_gather(expand_weight.T, ("seq", "tensor"), axis=0, tiled=True)
    weight_out = lax.all_gather(reduce_weight, ("seq", "tensor"), axis=0, tiled=True).T

    exchange = functools.partial(
        lax.all_to_all, axis_name="seq", split_axis=0, concat_axis=0, tiled=True
    )
    chunks = B // J
    front, back, done = {}, {}, {}
    mixed, ins, outs = {}, {}, {}
    result = None

    def do_front(k, dep=None):
        front[k] = exchange(first_pass(k, activations, first_factor, spectral, ns, dep))

    def do_second(k, deps=()):
        blocks = front[k].shape[1]
        x = front[k].reshape(ns * blocks, c // ns, J)
        mixed[k] = second_pass(x, second_factor, list(deps)).reshape(ns, blocks, c // ns, J)
        back[k] = exchange(mixed[k])

    def do_gate(k, deps=()):
        ins[k] = swap(gate(k, me, activations, back[k], scale, shift, nt, list(deps)))

    def do_mlp(k, deps=()):
        outs[k] = mlp(me, ins[k], weight_in, weight_out, list(deps))
        done[k] = swap(outs[k])

    do_front(0)
    do_front(1)
    do_second(0)
    do_front(2, front[1])
    do_second(1)
    do_front(3, back[0])
    do_gate(0)
    do_second(2)
    do_mlp(0)
    do_gate(1)
    do_second(3, [outs[0][0]])
    do_mlp(1)
    do_gate(2, [outs[0][0]])
    do_mlp(2)
    do_gate(3, [outs[1][0]])
    do_mlp(3)
    for k in range(chunks):
        result = place(k, me, done[k], result, activations.shape)
    return result


def solution(mesh):
    return jax.shard_map(
        functools.partial(on_device, mesh.shape["seq"], mesh.shape["tensor"]),
        mesh=mesh,
        in_specs=(
            P("tensor", "seq"),
            P(),
            P("tensor", "seq"),
            P(),
            P(),
            P(),
            P(None, ("seq", "tensor")),
            P(("seq", "tensor"), None),
        ),
        out_specs=P("tensor", "seq"),
        check_vma=False,
    )
```

```python
import functools

import jax
import jax.numpy as jnp
from jax import lax
from jax.experimental import pallas as pl
from jax.experimental.pallas import tpu as pltpu
from jax.sharding import PartitionSpec as P

B = 512
J = 128
epsilon = 1e-06
f32 = jnp.float32
bf16 = jnp.bfloat16
ANY = pl.BlockSpec(memory_space=pl.ANY)


def params(mib):
    return pltpu.CompilerParams(vmem_limit_bytes=mib * 2**20)


def first_pass(k, activations, first_factor, spectral, ns, dep):
    c, tokens = activations.shape
    blocks = tokens // B
    step = min(4, blocks)
    per = B // J
    deps = [] if dep is None else [dep]

    def kernel(act, factor, *rest):
        specs, out = rest[:step], rest[-1]
        for q in range(step):
            product = jnp.dot(act[:, q * B : (q + 1) * B], factor[...], preferred_element_type=f32)
            value = (product * specs[q][...]).astype(bf16)
            out[:, q] = value.reshape(ns, c // ns, J)

    def spec_at(q):
        return pl.BlockSpec((c, J), lambda i: (0, (i * step + q) * per + k))

    return pl.pallas_call(
        kernel,
        grid=(blocks // step,),
        in_specs=[
            pl.BlockSpec((c, step * B), lambda i: (0, i)),
            pl.BlockSpec((B, J), lambda i: (0, k)),
        ]
        + [spec_at(q) for q in range(step)]
        + [ANY] * len(deps),
        out_specs=pl.BlockSpec((ns, step, c // ns, J), lambda i: (0, i, 0, 0)),
        out_shape=jax.ShapeDtypeStruct((ns, blocks, c // ns, J), bf16),
        compiler_params=params(32),
        cost_estimate=pl.CostEstimate(
            flops=4 * c * blocks * B * J,
            bytes_accessed=2 * c * tokens + 6 * c * blocks * J,
            transcendentals=0,
        ),
    )(activations, first_factor, *[spectral] * step, *deps)


def second_pass(gathered, second_factor, deps):
    a, c, _ = gathered.shape
    cb = min(16, c)

    def kernel(x_ref, s_ref, *rest):
        out, x_wide, y_wide = rest[-3:]
        x_wide[...] = x_ref[...].astype(f32).reshape(a * cb, J)
        factor = s_ref[...]
        high = factor.astype(bf16)
        low = (factor - high.astype(f32)).astype(bf16)
        for i in range(0, cb, 2):
            x = jnp.concatenate(
                [x_wide[pl.ds(i + n, a, stride=cb), :] for n in range(2)], axis=1
            ).astype(bf16)
            y = jnp.dot(high, x, preferred_element_type=f32)
            y += jnp.dot(low, x, preferred_element_type=f32)
            for n in range(2):
                y_wide[pl.ds(i + n, a, stride=cb), :] = y[:, n * J : (n + 1) * J]
        out[...] = y_wide[...].reshape(a, cb, J).astype(bf16)

    return pl.pallas_call(
        kernel,
        grid=(c // cb,),
        in_specs=[
            pl.BlockSpec((a, cb, J), lambda i: (0, i, 0)),
            pl.BlockSpec((a, a), lambda i: (0, 0)),
        ]
        + [ANY] * len(deps),
        out_specs=pl.BlockSpec((a, cb, J), lambda i: (0, i, 0)),
        out_shape=jax.ShapeDtypeStruct((a, c, J), bf16),
        scratch_shapes=[pltpu.VMEM((a * cb, J), f32), pltpu.VMEM((a * cb, J), f32)],
        compiler_params=params(32),
        cost_estimate=pl.CostEstimate(
            flops=8 * a * a * c * J, bytes_accessed=4 * a * c * J, transcendentals=0
        ),
    )(gathered, second_factor, *deps)


def gate(k, me, activations, returned, scale, shift, nt, deps):
    c, tokens = activations.shape
    ns, blocks, ci, _ = returned.shape
    mine = blocks // nt
    step = min(2, mine)
    steps = mine // step

    def kernel(me_ref, *rest):
        acts, rets = rest[:nt], rest[nt : 2 * nt]
        scale_ref, shift_ref = rest[2 * nt : 2 * nt + 2]
        outs = rest[-nt:]
        for s in range(nt):
            for q in range(step):
                x = acts[s][:, q * B + k * J : q * B + (k + 1) * J].astype(f32)
                mixed = rets[s][:, q].reshape(c, J).astype(f32)
                gating = jax.nn.sigmoid(x * scale_ref[...] + shift_ref[...])
                outs[s][:, q * J : (q + 1) * J] = (x + gating * mixed).astype(bf16)

    def act_at(s):
        return pl.BlockSpec((c, step * B), lambda i, me: (0, (me[0] ^ s) * steps + i))

    def ret_at(s):
        return pl.BlockSpec(
            (ns, step, ci, J), lambda i, me: (0, (me[0] ^ s) * steps + i, 0, 0)
        )

    column = pl.BlockSpec((c, 1), lambda i, me: (0, 0))
    return pl.pallas_call(
        kernel,
        grid_spec=pltpu.PrefetchScalarGridSpec(
            num_scalar_prefetch=1,
            grid=(steps,),
            in_specs=[act_at(s) for s in range(nt)]
            + [ret_at(s) for s in range(nt)]
            + [column, column]
            + [ANY] * len(deps),
            out_specs=[pl.BlockSpec((c, step * J), lambda i, me: (0, i))] * nt,
        ),
        out_shape=[jax.ShapeDtypeStruct((c, mine * J), bf16)] * nt,
        compiler_params=params(32),
        cost_estimate=pl.CostEstimate(
            flops=8 * c * blocks * J,
            bytes_accessed=2 * c * tokens + 4 * c * blocks * J,
            transcendentals=c * blocks * J,
        ),
    )(me, *[activations] * nt, *[returned] * nt, scale, shift, *deps)


def mlp(me, slots, pieces_in, pieces_out, deps):
    nt = len(slots)
    c, tokens = slots[0].shape
    hb, full = pieces_in[0].shape
    n = len(pieces_in)
    tile = min(256, tokens)

    def kernel(me_ref, *rest):
        xs, w1s, w2s = rest[:nt], rest[nt : nt + n], rest[nt + n : nt + 2 * n]
        outs = rest[-nt - 5 : -5]
        normed, total, w1, w2, sems = rest[-5:]
        step = pl.program_id(0)

        def fetch(piece, slot):
            return (
                pltpu.make_async_copy(w1s[piece], w1.at[slot], sems.at[0, slot]),
                pltpu.make_async_copy(w2s[piece], w2.at[slot], sems.at[1, slot]),
            )

        def start(piece):
            for copy in fetch(piece, piece % 2):
                copy.start()

        @pl.when(step == 0)
        def _():
            start(0)
            squares = jnp.zeros((1, tokens), f32)
            for s in range(nt):
                x = xs[s][...].astype(f32)
                squares += jnp.sum(x * x, axis=0, keepdims=True)
            scale = lax.rsqrt(squares / full + epsilon)
            for s in range(nt):
                at = pl.multiple_of((me_ref[0] ^ s) * c, c)
                normed[pl.ds(at, c), :] = (xs[s][...].astype(f32) * scale).astype(bf16)
            total[...] = jnp.zeros_like(total)

        for piece in range(1, n):
            pl.when(step == piece - 1)(functools.partial(start, piece))
        slot = lax.rem(step, 2)
        for copy in fetch(0, slot):
            copy.wait()

        for t in range(0, tokens, tile):
            x = jnp.dot(w1[slot], normed[:, t : t + tile], preferred_element_type=f32)
            h = jax.nn.gelu(x).astype(bf16)
            total[:, t : t + tile] += jnp.dot(w2[slot], h, preferred_element_type=f32)

        @pl.when(step == n - 1)
        def _():
            for s in range(nt):
                at = pl.multiple_of((me_ref[0] ^ s) * c, c)
                outs[s][...] = (xs[s][...].astype(f32) + total[pl.ds(at, c), :]).astype(bf16)

    whole = pl.BlockSpec((c, tokens), lambda i, me: (0, 0))
    return pl.pallas_call(
        kernel,
        grid_spec=pltpu.PrefetchScalarGridSpec(
            num_scalar_prefetch=1,
            grid=(n,),
            in_specs=[whole] * nt + [ANY] * (2 * n + len(deps)),
            out_specs=[whole] * nt,
            scratch_shapes=[
                pltpu.VMEM((full, tokens), bf16),
                pltpu.VMEM((full, tokens), f32),
                pltpu.VMEM((2, hb, full), bf16),
                pltpu.VMEM((2, full, hb), bf16),
                pltpu.SemaphoreType.DMA((2, 2)),
            ],
        ),
        out_shape=[jax.ShapeDtypeStruct((c, tokens), bf16)] * nt,
        compiler_params=params(40),
        cost_estimate=pl.CostEstimate(
            flops=4 * full * hb * n * tokens,
            bytes_accessed=4 * full * hb * n + 4 * full * tokens,
            transcendentals=hb * n * tokens,
        ),
    )(me, *slots, *pieces_in, *pieces_out, *deps)


def place(k, me, slots, result, shape):
    nt = len(slots)
    c, tokens = slots[0].shape
    mine = tokens // J
    given = [] if result is None else [result]

    def kernel(me_ref, *rest):
        ys, out, sems = rest[:nt], rest[-2], rest[-1]
        copies = []
        for s in range(nt):
            for q in range(mine):
                at = pl.multiple_of(((me_ref[0] ^ s) * mine + q) * B + k * J, J)
                copies.append(
                    pltpu.make_async_copy(
                        ys[s].at[:, q * J : (q + 1) * J],
                        out.at[:, pl.ds(at, J)],
                        sems.at[s * mine + q],
                    )
                )
        for copy in copies:
            copy.start()
        for copy in copies:
            copy.wait()

    return pl.pallas_call(
        kernel,
        in_specs=[pl.BlockSpec(memory_space=pltpu.SMEM)]
        + [pl.BlockSpec(memory_space=pltpu.VMEM)] * nt
        + [ANY] * len(given),
        out_specs=ANY,
        out_shape=jax.ShapeDtypeStruct(shape, bf16),
        scratch_shapes=[pltpu.SemaphoreType.DMA((nt * mine,))],
        compiler_params=params(16),
        input_output_aliases={1 + nt: 0} if given else {},
        cost_estimate=pl.CostEstimate(
            flops=0, bytes_accessed=4 * c * tokens * nt, transcendentals=0
        ),
    )(me, *slots, *given)


def swap(slots):
    n = len(slots)
    return [slots[0]] + [
        lax.ppermute(slots[s], "tensor", [(i, i ^ s) for i in range(n)]) for s in range(1, n)
    ]


def after(x, *deps):
    return pl.pallas_call(
        lambda *refs: None,
        in_specs=[ANY] * (1 + len(deps)),
        out_specs=ANY,
        out_shape=jax.ShapeDtypeStruct(x.shape, x.dtype),
        input_output_aliases={0: 0},
    )(x, *deps)


def gather_weights(ns, nt, expand_weight, reduce_weight):
    def flip(x, axis, bit):
        n = ns if axis == "seq" else nt
        return lax.ppermute(x, axis, [(i, i ^ bit) for i in range(n)])

    rows, full = reduce_weight.shape
    both = jnp.stack([expand_weight.T, reduce_weight])[None]
    bit = 2
    while bit < ns:
        both = jnp.concatenate([both, flip(both, "seq", bit)])
        bit *= 2
    bits = [1 << i for i in range(nt.bit_length() - 1)]
    column = [both[:, 0].reshape(-1, full), both[:, 1].reshape(-1, full).T]
    found = []
    for start, order in zip(column, (bits, bits[::-1])):
        pieces = {0: start}
        for bit in order:
            pieces |= {s ^ bit: flip(x, "tensor", bit) for s, x in pieces.items()}
        found.append([pieces[s] for s in range(nt)])
    other = [[flip(x, "seq", 1) for x in pieces] for pieces in found]
    return both, found[0], found[1], found[0] + other[0], found[1] + other[1]


def on_device(
    ns,
    nt,
    activations,
    first_factor,
    spectral,
    second_factor,
    gate_scale,
    gate_shift,
    expand_weight,
    reduce_weight,
):
    c = activations.shape[0]
    at = lax.axis_index("tensor")
    me = at.astype(jnp.int32).reshape(1)
    scale = lax.dynamic_slice_in_dim(gate_scale, at * c, c)[:, None]
    shift = lax.dynamic_slice_in_dim(gate_shift, at * c, c)[:, None]
    both, near_in, near_out, pieces_in, pieces_out = gather_weights(
        ns, nt, expand_weight, reduce_weight
    )

    def exchange(x):
        return lax.all_to_all(x, "seq", split_axis=0, concat_axis=0, tiled=True)

    def first(k, dep=None):
        return first_pass(k, activations, first_factor, spectral, ns, dep)

    def second(front, deps=()):
        blocks = front.shape[1]
        x = front.reshape(ns * blocks, c // ns, J)
        return second_pass(x, second_factor, list(deps)).reshape(ns, blocks, c // ns, J)

    def gated(k, back, deps=()):
        return gate(k, me, activations, back, scale, shift, nt, list(deps))

    def layer(slots, deps=()):
        return mlp(me, slots, pieces_in, pieces_out, list(deps))

    front0 = exchange(first(0))
    front1 = exchange(first(1))
    back0 = exchange(second(front0))
    front2 = exchange(first(2, both))
    back1 = exchange(second(front1))
    sent3 = first(3, front1)
    in0 = swap(gated(0, back0, near_in + near_out))
    mixed2 = second(front2)
    out0 = layer(in0, [front2])
    front3 = exchange(after(sent3, out0[0], mixed2))
    in1 = swap(gated(1, back1, [out0[0]]))
    back2 = exchange(mixed2)
    mixed3 = second(front3)
    out1 = layer(in1, [front3])
    back3 = exchange(after(mixed3, out1[0]))
    done0 = swap(out0)
    in2 = swap(gated(2, back2, [out1[0]]))
    done1 = swap(out1)
    gate3 = gated(3, back3)
    in3 = swap(gate3)
    out2 = layer(in2, [gate3[0]])
    done2 = swap(out2)
    out3 = layer(in3)
    done3 = swap(out3)
    result = None
    for k, done in enumerate((done0, done1, done2, done3)):
        result = place(k, me, done, result, activations.shape)
    return result


def solution(mesh):
    return jax.shard_map(
        functools.partial(on_device, mesh.shape["seq"], mesh.shape["tensor"]),
        mesh=mesh,
        in_specs=(
            P("tensor", "seq"),
            P(),
            P("tensor", "seq"),
            P(),
            P(),
            P(),
            P(None, ("seq", "tensor")),
            P(("seq", "tensor"), None),
        ),
        out_specs=P("tensor", "seq"),
        check_vma=False,
    )
```

```python
import functools

import jax
import jax.numpy as jnp
from jax import lax
from jax.experimental import pallas as pl
from jax.experimental.pallas import tpu as pltpu
from jax.sharding import PartitionSpec as P

B = 512
J = 128
epsilon = 1e-06
f32 = jnp.float32
bf16 = jnp.bfloat16
ANY = pl.BlockSpec(memory_space=pl.ANY)


def params(mib):
    return pltpu.CompilerParams(vmem_limit_bytes=mib * 2**20)


def first_pass(at, n, activations, first_factor, spectral, ns, deps=()):
    c, tokens = activations.shape
    blocks = tokens // B
    step = min(4, blocks)
    wide = n * J
    per = B // wide

    def kernel(act, factor, *rest):
        specs, out = rest[:step], rest[-1]
        for q in range(step):
            product = jnp.dot(act[:, q * B : (q + 1) * B], factor[...], preferred_element_type=f32)
            value = (product * specs[q][...]).astype(bf16)
            for m in range(n):
                out[:, m, q] = value[:, m * J : (m + 1) * J].reshape(ns, c // ns, J)

    def spec_at(q):
        return pl.BlockSpec((c, wide), lambda i: (0, (i * step + q) * per + at))

    return pl.pallas_call(
        kernel,
        grid=(blocks // step,),
        in_specs=[
            pl.BlockSpec((c, step * B), lambda i: (0, i)),
            pl.BlockSpec((B, wide), lambda i: (0, at)),
        ]
        + [spec_at(q) for q in range(step)]
        + [ANY] * len(deps),
        out_specs=pl.BlockSpec((ns, n, step, c // ns, J), lambda i: (0, 0, i, 0, 0)),
        out_shape=jax.ShapeDtypeStruct((ns, n, blocks, c // ns, J), bf16),
        compiler_params=params(32),
        cost_estimate=pl.CostEstimate(
            flops=2 * c * blocks * B * wide,
            bytes_accessed=2 * c * tokens + 6 * c * blocks * wide,
            transcendentals=0,
        ),
    )(activations, first_factor, *[spectral] * step, *deps)


def second_pass(gathered, m, second_factor, deps=()):
    ns, _, blocks, c, _ = gathered.shape
    a = ns * blocks
    cb = min(16, c)

    def kernel(x_ref, s_ref, *rest):
        out, x_wide, y_wide = rest[-3:]
        x_wide[...] = x_ref[...].astype(f32).reshape(a * cb, J)
        factor = s_ref[...]
        high = factor.astype(bf16)
        low = (factor - high.astype(f32)).astype(bf16)
        for i in range(0, cb, 2):
            x = jnp.concatenate(
                [x_wide[pl.ds(i + h, a, stride=cb), :] for h in range(2)], axis=1
            ).astype(bf16)
            y = jnp.dot(high, x, preferred_element_type=f32)
            y += jnp.dot(low, x, preferred_element_type=f32)
            for h in range(2):
                y_wide[pl.ds(i + h, a, stride=cb), :] = y[:, h * J : (h + 1) * J]
        out[...] = y_wide[...].reshape(ns, blocks, cb, J).astype(bf16)

    return pl.pallas_call(
        kernel,
        grid=(c // cb,),
        in_specs=[
            pl.BlockSpec((ns, 1, blocks, cb, J), lambda i: (0, m, 0, i, 0)),
            pl.BlockSpec((a, a), lambda i: (0, 0)),
        ]
        + [ANY] * len(deps),
        out_specs=pl.BlockSpec((ns, blocks, cb, J), lambda i: (0, 0, i, 0)),
        out_shape=jax.ShapeDtypeStruct((ns, blocks, c, J), bf16),
        scratch_shapes=[pltpu.VMEM((a * cb, J), f32), pltpu.VMEM((a * cb, J), f32)],
        compiler_params=params(32),
        cost_estimate=pl.CostEstimate(
            flops=8 * a * a * c * J, bytes_accessed=4 * a * c * J, transcendentals=0
        ),
    )(gathered, second_factor, *deps)


def gate(k, me, activations, returned, scale, shift, nt, deps):
    c, tokens = activations.shape
    ns, blocks, ci, _ = returned.shape
    mine = blocks // nt
    step = min(2, mine)
    steps = mine // step

    def kernel(me_ref, *rest):
        acts, rets = rest[:nt], rest[nt : 2 * nt]
        scale_ref, shift_ref = rest[2 * nt : 2 * nt + 2]
        outs = rest[-nt:]
        for s in range(nt):
            for q in range(step):
                x = acts[s][:, q * B + k * J : q * B + (k + 1) * J].astype(f32)
                mixed = rets[s][:, q].reshape(c, J).astype(f32)
                gating = jax.nn.sigmoid(x * scale_ref[...] + shift_ref[...])
                outs[s][:, q * J : (q + 1) * J] = (x + gating * mixed).astype(bf16)

    def act_at(s):
        return pl.BlockSpec((c, step * B), lambda i, me: (0, (me[0] ^ s) * steps + i))

    def ret_at(s):
        return pl.BlockSpec(
            (ns, step, ci, J), lambda i, me: (0, (me[0] ^ s) * steps + i, 0, 0)
        )

    column = pl.BlockSpec((c, 1), lambda i, me: (0, 0))
    return pl.pallas_call(
        kernel,
        grid_spec=pltpu.PrefetchScalarGridSpec(
            num_scalar_prefetch=1,
            grid=(steps,),
            in_specs=[act_at(s) for s in range(nt)]
            + [ret_at(s) for s in range(nt)]
            + [column, column]
            + [ANY] * len(deps),
            out_specs=[pl.BlockSpec((c, step * J), lambda i, me: (0, i))] * nt,
        ),
        out_shape=[jax.ShapeDtypeStruct((c, mine * J), bf16)] * nt,
        compiler_params=params(32),
        cost_estimate=pl.CostEstimate(
            flops=8 * c * blocks * J,
            bytes_accessed=2 * c * tokens + 4 * c * blocks * J,
            transcendentals=c * blocks * J,
        ),
    )(me, *[activations] * nt, *[returned] * nt, scale, shift, *deps)


def mlp(me, slots, halves_in, halves_out, deps):
    nt = len(slots)
    c, tokens = slots[0].shape
    half, hb, full = halves_in[0].shape
    n = 2 * half
    tile = min(256, tokens)

    def kernel(me_ref, *rest):
        xs, w1s, w2s = rest[:nt], rest[nt : nt + 2], rest[nt + 2 : nt + 4]
        outs = rest[-nt - 5 : -5]
        normed, total, w1, w2, sems = rest[-5:]
        step = pl.program_id(0)

        def fetch(piece, slot):
            return (
                pltpu.make_async_copy(
                    w1s[piece // half].at[piece % half], w1.at[slot], sems.at[0, slot]
                ),
                pltpu.make_async_copy(
                    w2s[piece // half].at[piece % half], w2.at[slot], sems.at[1, slot]
                ),
            )

        def start(piece):
            for copy in fetch(piece, piece % 2):
                copy.start()

        @pl.when(step == 0)
        def _():
            start(0)
            squares = jnp.zeros((1, tokens), f32)
            for s in range(nt):
                x = xs[s][...].astype(f32)
                squares += jnp.sum(x * x, axis=0, keepdims=True)
            scale = lax.rsqrt(squares / full + epsilon)
            for s in range(nt):
                at = pl.multiple_of((me_ref[0] ^ s) * c, c)
                normed[pl.ds(at, c), :] = (xs[s][...].astype(f32) * scale).astype(bf16)
            total[...] = jnp.zeros_like(total)

        for piece in range(1, n):
            pl.when(step == piece - 1)(functools.partial(start, piece))
        slot = lax.rem(step, 2)
        for copy in fetch(0, slot):
            copy.wait()

        def expand(t):
            return jnp.dot(w1[slot], normed[:, t : t + tile], preferred_element_type=f32)

        ahead = expand(0)
        for t in range(0, tokens, tile):
            x = ahead
            if t + tile < tokens:
                ahead = expand(t + tile)
            h = jax.nn.gelu(x).astype(bf16)
            total[:, t : t + tile] += jnp.dot(w2[slot], h, preferred_element_type=f32)

        @pl.when(step == n - 1)
        def _():
            for s in range(nt):
                at = pl.multiple_of((me_ref[0] ^ s) * c, c)
                outs[s][...] = (xs[s][...].astype(f32) + total[pl.ds(at, c), :]).astype(bf16)

    whole = pl.BlockSpec((c, tokens), lambda i, me: (0, 0))
    return pl.pallas_call(
        kernel,
        grid_spec=pltpu.PrefetchScalarGridSpec(
            num_scalar_prefetch=1,
            grid=(n,),
            in_specs=[whole] * nt + [ANY] * (4 + len(deps)),
            out_specs=[whole] * nt,
            scratch_shapes=[
                pltpu.VMEM((full, tokens), bf16),
                pltpu.VMEM((full, tokens), f32),
                pltpu.VMEM((2, hb, full), bf16),
                pltpu.VMEM((2, full, hb), bf16),
                pltpu.SemaphoreType.DMA((2, 2)),
            ],
        ),
        out_shape=[jax.ShapeDtypeStruct((c, tokens), bf16)] * nt,
        compiler_params=params(40),
        cost_estimate=pl.CostEstimate(
            flops=4 * full * hb * n * tokens,
            bytes_accessed=4 * full * hb * n + 4 * full * tokens,
            transcendentals=hb * n * tokens,
        ),
    )(me, *slots, *halves_in, *halves_out, *deps)


def place(k, me, slots, result, shape):
    nt = len(slots)
    c, tokens = slots[0].shape
    mine = tokens // J
    given = [] if result is None else [result]

    def kernel(me_ref, *rest):
        ys, out, sems = rest[:nt], rest[-2], rest[-1]
        copies = []
        for s in range(nt):
            for q in range(mine):
                at = pl.multiple_of(((me_ref[0] ^ s) * mine + q) * B + k * J, J)
                copies.append(
                    pltpu.make_async_copy(
                        ys[s].at[:, q * J : (q + 1) * J],
                        out.at[:, pl.ds(at, J)],
                        sems.at[s * mine + q],
                    )
                )
        for copy in copies:
            copy.start()
        for copy in copies:
            copy.wait()

    return pl.pallas_call(
        kernel,
        in_specs=[pl.BlockSpec(memory_space=pltpu.SMEM)]
        + [pl.BlockSpec(memory_space=pltpu.VMEM)] * nt
        + [ANY] * len(given),
        out_specs=ANY,
        out_shape=jax.ShapeDtypeStruct(shape, bf16),
        scratch_shapes=[pltpu.SemaphoreType.DMA((nt * mine,))],
        compiler_params=params(16),
        input_output_aliases={1 + nt: 0} if given else {},
        cost_estimate=pl.CostEstimate(
            flops=0, bytes_accessed=4 * c * tokens * nt, transcendentals=0
        ),
    )(me, *slots, *given)


def swap(slots):
    n = len(slots)
    return [slots[0]] + [
        lax.ppermute(slots[s], "tensor", [(i, i ^ s) for i in range(n)]) for s in range(1, n)
    ]


def after(x, *deps):
    return pl.pallas_call(
        lambda *refs: None,
        in_specs=[ANY] * (1 + len(deps)),
        out_specs=ANY,
        out_shape=jax.ShapeDtypeStruct(x.shape, x.dtype),
        input_output_aliases={0: 0},
    )(x, *deps)


def flip(x, axis, n, bit):
    return lax.ppermute(x, axis, [(i, i ^ bit) for i in range(n)])


def gather_along(ns, both):
    got = [flip(both, "seq", ns, 2)]
    both = jnp.concatenate([both, got[0]])
    bit = 4
    if ns % 8 == 0:
        middle = [i for i in range(ns) if ((i >> 1) ^ (i >> 2)) & 1]
        got.append(lax.ppermute(both, "seq", [(i, i ^ 6) for i in middle]))
        got.append(lax.ppermute(got[1], "seq", [(i, i ^ 2) for i in middle]))
        both = jnp.concatenate([both, got[1] + got[2]])
        bit = 8
    while bit < ns:
        got.append(flip(both, "seq", ns, bit))
        both = jnp.concatenate([both, got[-1]])
        bit *= 2
    return both, got


def gather_across(nt, start, order):
    pieces = {0: start}
    for bit in order:
        pieces |= {s ^ bit: flip(x, "tensor", nt, bit) for s, x in pieces.items()}
    return pieces


def on_device(
    ns,
    nt,
    activations,
    first_factor,
    spectral,
    second_factor,
    gate_scale,
    gate_shift,
    expand_weight,
    reduce_weight,
):
    c = activations.shape[0]
    full = reduce_weight.shape[1]
    at = lax.axis_index("tensor")
    me = at.astype(jnp.int32).reshape(1)
    scale = lax.dynamic_slice_in_dim(gate_scale, at * c, c)[:, None]
    shift = lax.dynamic_slice_in_dim(gate_shift, at * c, c)[:, None]
    both, got = gather_along(ns, jnp.stack([expand_weight.T, reduce_weight])[None])
    bits = [1 << i for i in range(nt.bit_length() - 1)]
    near_in = gather_across(nt, both[:, 0].reshape(-1, full), bits)
    near_out = gather_across(nt, both[:, 1].reshape(-1, full).T, bits[::-1])
    halves_in = [jnp.stack([near_in[s] for s in range(nt)])]
    halves_in.append(flip(halves_in[0], "seq", ns, 1))
    halves_out = [jnp.stack([near_out[s] for s in range(nt)])]
    halves_out.append(flip(halves_out[0], "seq", ns, 1))

    def exchange(x):
        return lax.all_to_all(x, "seq", split_axis=0, concat_axis=0, tiled=True)

    def first(at, n, deps=()):
        return first_pass(at, n, activations, first_factor, spectral, ns, deps)

    def second(front, m, deps=()):
        return second_pass(front, m, second_factor, deps)

    def gated(k, back, deps=()):
        return gate(k, me, activations, back, scale, shift, nt, list(deps))

    def layer(slots, deps=()):
        return mlp(me, slots, halves_in, halves_out, list(deps))

    front01 = exchange(after(first(0, 2), got[0]))
    front23 = exchange(after(first(1, 2, [got[1]]), got[-1]))
    mixed0 = second(front01, 0, [near_in[bits[0]], near_out[bits[-1]]])
    mixed1 = second(front01, 1)
    back0 = exchange(mixed0)
    mixed2 = second(front23, 0, [halves_in[0], halves_out[0]])
    back1 = exchange(mixed1)
    mixed3 = second(front23, 1, [halves_in[1], halves_out[1]])
    gate0 = gated(0, back0)
    in0 = swap(gate0)
    back2 = exchange(after(mixed2, gate0[0]))
    gate1 = gated(1, back1)
    in1 = swap(gate1)
    out0 = layer(in0, [gate1[0]])
    done0 = swap(out0)
    back3 = exchange(after(mixed3, out0[0]))
    gate2 = gated(2, back2)
    in2 = swap(gate2)
    out1 = layer(in1, [gate2[0]])
    done1 = swap(out1)
    result = place(0, me, done0, None, activations.shape)
    gate3 = gated(3, back3, [out1[0], result])
    in3 = swap(gate3)
    out2 = layer(in2, [gate3[0]])
    done2 = swap(out2)
    result = place(1, me, done1, result, activations.shape)
    out3 = layer(in3, [out2[0], result])
    done3 = swap(out3)
    result = place(2, me, done2, result, activations.shape)
    return place(3, me, done3, result, activations.shape)


def solution(mesh):
    return jax.shard_map(
        functools.partial(on_device, mesh.shape["seq"], mesh.shape["tensor"]),
        mesh=mesh,
        in_specs=(
            P("tensor", "seq"),
            P(),
            P("tensor", "seq"),
            P(),
            P(),
            P(),
            P(None, ("seq", "tensor")),
            P(("seq", "tensor"), None),
        ),
        out_specs=P("tensor", "seq"),
        check_vma=False,
    )
```

```python
import functools

import jax
import jax.numpy as jnp
from jax import lax
from jax.experimental import pallas as pl
from jax.experimental.pallas import tpu as pltpu
from jax.sharding import PartitionSpec as P

B = 512
J = 128
epsilon = 1e-06
f32 = jnp.float32
bf16 = jnp.bfloat16
ANY = pl.BlockSpec(memory_space=pl.ANY)


def params(mib):
    return pltpu.CompilerParams(vmem_limit_bytes=mib * 2**20)


def first_pass(at, n, activations, first_factor, spectral, ns, deps=()):
    c, tokens = activations.shape
    blocks = tokens // B
    step = min(4, blocks)
    wide = n * J
    per = B // wide

    def kernel(act, factor, *rest):
        specs, out = rest[:step], rest[-1]
        for q in range(step):
            product = jnp.dot(act[:, q * B : (q + 1) * B], factor[...], preferred_element_type=f32)
            value = (product * specs[q][...]).astype(bf16)
            for m in range(n):
                out[:, m, q] = value[:, m * J : (m + 1) * J].reshape(ns, c // ns, J)

    def spec_at(q):
        return pl.BlockSpec((c, wide), lambda i: (0, (i * step + q) * per + at))

    return pl.pallas_call(
        kernel,
        grid=(blocks // step,),
        in_specs=[
            pl.BlockSpec((c, step * B), lambda i: (0, i)),
            pl.BlockSpec((B, wide), lambda i: (0, at)),
        ]
        + [spec_at(q) for q in range(step)]
        + [ANY] * len(deps),
        out_specs=pl.BlockSpec((ns, n, step, c // ns, J), lambda i: (0, 0, i, 0, 0)),
        out_shape=jax.ShapeDtypeStruct((ns, n, blocks, c // ns, J), bf16),
        compiler_params=params(32),
        cost_estimate=pl.CostEstimate(
            flops=2 * c * blocks * B * wide,
            bytes_accessed=2 * c * tokens + 6 * c * blocks * wide,
            transcendentals=0,
        ),
    )(activations, first_factor, *[spectral] * step, *deps)


def second_pass(gathered, m, second_factor, groups, deps=()):
    ns, _, blocks, c, _ = gathered.shape
    a = ns * blocks
    cb = min(16, c)
    part = blocks // groups

    def kernel(x_ref, s_ref, *rest):
        outs, (x_wide, y_wide) = rest[-groups - 2 : -2], rest[-2:]
        x_wide[...] = x_ref[...].astype(f32).reshape(a * cb, J)
        factor = s_ref[...]
        high = factor.astype(bf16)
        low = (factor - high.astype(f32)).astype(bf16)
        for i in range(0, cb, 2):
            x = jnp.concatenate(
                [x_wide[pl.ds(i + h, a, stride=cb), :] for h in range(2)], axis=1
            ).astype(bf16)
            y = jnp.dot(high, x, preferred_element_type=f32)
            y += jnp.dot(low, x, preferred_element_type=f32)
            for h in range(2):
                y_wide[pl.ds(i + h, a, stride=cb), :] = y[:, h * J : (h + 1) * J]
        y = y_wide[...].reshape(ns, blocks, cb, J)
        for g in range(groups):
            outs[g][...] = y[:, g * part : (g + 1) * part].astype(bf16)

    return pl.pallas_call(
        kernel,
        grid=(c // cb,),
        in_specs=[
            pl.BlockSpec((ns, 1, blocks, cb, J), lambda i: (0, m, 0, i, 0)),
            pl.BlockSpec((a, a), lambda i: (0, 0)),
        ]
        + [ANY] * len(deps),
        out_specs=[pl.BlockSpec((ns, part, cb, J), lambda i: (0, 0, i, 0))] * groups,
        out_shape=[jax.ShapeDtypeStruct((ns, part, c, J), bf16)] * groups,
        scratch_shapes=[pltpu.VMEM((a * cb, J), f32), pltpu.VMEM((a * cb, J), f32)],
        compiler_params=params(32),
        cost_estimate=pl.CostEstimate(
            flops=8 * a * a * c * J, bytes_accessed=4 * a * c * J, transcendentals=0
        ),
    )(gathered, second_factor, *deps)


def gate(k, group, me, activations, returned, scale, shift, nt, deps):
    c, tokens = activations.shape
    ns, blocks, ci, _ = returned.shape
    mine = blocks // nt
    step = min(2, mine)
    steps = mine // step
    begin = group * blocks // step

    def kernel(me_ref, *rest):
        acts, rets = rest[:nt], rest[nt : 2 * nt]
        scale_ref, shift_ref = rest[2 * nt : 2 * nt + 2]
        outs = rest[-nt:]
        for s in range(nt):
            for q in range(step):
                x = acts[s][:, q * B + k * J : q * B + (k + 1) * J].astype(f32)
                mixed = rets[s][:, q].reshape(c, J).astype(f32)
                gating = jax.nn.sigmoid(x * scale_ref[...] + shift_ref[...])
                outs[s][:, q * J : (q + 1) * J] = (x + gating * mixed).astype(bf16)

    def act_at(s):
        return pl.BlockSpec((c, step * B), lambda i, me: (0, begin + (me[0] ^ s) * steps + i))

    def ret_at(s):
        return pl.BlockSpec(
            (ns, step, ci, J), lambda i, me: (0, (me[0] ^ s) * steps + i, 0, 0)
        )

    column = pl.BlockSpec((c, 1), lambda i, me: (0, 0))
    return pl.pallas_call(
        kernel,
        grid_spec=pltpu.PrefetchScalarGridSpec(
            num_scalar_prefetch=1,
            grid=(steps,),
            in_specs=[act_at(s) for s in range(nt)]
            + [ret_at(s) for s in range(nt)]
            + [column, column]
            + [ANY] * len(deps),
            out_specs=[pl.BlockSpec((c, step * J), lambda i, me: (0, i))] * nt,
        ),
        out_shape=[jax.ShapeDtypeStruct((c, mine * J), bf16)] * nt,
        compiler_params=params(32),
        cost_estimate=pl.CostEstimate(
            flops=8 * c * blocks * J,
            bytes_accessed=2 * c * tokens + 4 * c * blocks * J,
            transcendentals=c * blocks * J,
        ),
    )(me, *[activations] * nt, *[returned] * nt, scale, shift, *deps)


def mlp(me, slots, halves_in, halves_out, deps):
    nt = len(slots)
    c, tokens = slots[0].shape
    half, hb, full = halves_in[0].shape
    n = 2 * half
    tile = min(256, tokens)

    def kernel(me_ref, *rest):
        xs, w1s, w2s = rest[:nt], rest[nt : nt + 2], rest[nt + 2 : nt + 4]
        outs = rest[-nt - 5 : -5]
        normed, total, w1, w2, sems = rest[-5:]
        step = pl.program_id(0)

        def fetch(piece, slot):
            return (
                pltpu.make_async_copy(
                    w1s[piece // half].at[piece % half], w1.at[slot], sems.at[0, slot]
                ),
                pltpu.make_async_copy(
                    w2s[piece // half].at[piece % half], w2.at[slot], sems.at[1, slot]
                ),
            )

        def start(piece):
            for copy in fetch(piece, piece % 2):
                copy.start()

        @pl.when(step == 0)
        def _():
            start(0)
            squares = jnp.zeros((1, tokens), f32)
            for s in range(nt):
                x = xs[s][...].astype(f32)
                squares += jnp.sum(x * x, axis=0, keepdims=True)
            scale = lax.rsqrt(squares / full + epsilon)
            for s in range(nt):
                at = pl.multiple_of((me_ref[0] ^ s) * c, c)
                normed[pl.ds(at, c), :] = (xs[s][...].astype(f32) * scale).astype(bf16)
            total[...] = jnp.zeros_like(total)

        for piece in range(1, n):
            pl.when(step == piece - 1)(functools.partial(start, piece))
        slot = lax.rem(step, 2)
        for copy in fetch(0, slot):
            copy.wait()

        def expand(t):
            return jnp.dot(w1[slot], normed[:, t : t + tile], preferred_element_type=f32)

        ahead = expand(0)
        for t in range(0, tokens, tile):
            x = ahead
            if t + tile < tokens:
                ahead = expand(t + tile)
            h = jax.nn.gelu(x).astype(bf16)
            total[:, t : t + tile] += jnp.dot(w2[slot], h, preferred_element_type=f32)

        @pl.when(step == n - 1)
        def _():
            for s in range(nt):
                at = pl.multiple_of((me_ref[0] ^ s) * c, c)
                outs[s][...] = (xs[s][...].astype(f32) + total[pl.ds(at, c), :]).astype(bf16)

    whole = pl.BlockSpec((c, tokens), lambda i, me: (0, 0))
    return pl.pallas_call(
        kernel,
        grid_spec=pltpu.PrefetchScalarGridSpec(
            num_scalar_prefetch=1,
            grid=(n,),
            in_specs=[whole] * nt + [ANY] * (4 + len(deps)),
            out_specs=[whole] * nt,
            scratch_shapes=[
                pltpu.VMEM((full, tokens), bf16),
                pltpu.VMEM((full, tokens), f32),
                pltpu.VMEM((2, hb, full), bf16),
                pltpu.VMEM((2, full, hb), bf16),
                pltpu.SemaphoreType.DMA((2, 2)),
            ],
        ),
        out_shape=[jax.ShapeDtypeStruct((c, tokens), bf16)] * nt,
        compiler_params=params(40),
        cost_estimate=pl.CostEstimate(
            flops=4 * full * hb * n * tokens,
            bytes_accessed=4 * full * hb * n + 4 * full * tokens,
            transcendentals=hb * n * tokens,
        ),
    )(me, *slots, *halves_in, *halves_out, *deps)


def place(k, group, me, slots, result, shape):
    nt = len(slots)
    c, tokens = slots[0].shape
    mine = tokens // J
    given = [] if result is None else [result]

    def kernel(me_ref, *rest):
        ys, out, sems = rest[:nt], rest[-2], rest[-1]
        copies = []
        for s in range(nt):
            for q in range(mine):
                block = group * nt * mine + (me_ref[0] ^ s) * mine + q
                at = pl.multiple_of(block * B + k * J, J)
                copies.append(
                    pltpu.make_async_copy(
                        ys[s].at[:, q * J : (q + 1) * J],
                        out.at[:, pl.ds(at, J)],
                        sems.at[s * mine + q],
                    )
                )
        for copy in copies:
            copy.start()
        for copy in copies:
            copy.wait()

    return pl.pallas_call(
        kernel,
        in_specs=[pl.BlockSpec(memory_space=pltpu.SMEM)]
        + [pl.BlockSpec(memory_space=pltpu.VMEM)] * nt
        + [ANY] * len(given),
        out_specs=ANY,
        out_shape=jax.ShapeDtypeStruct(shape, bf16),
        scratch_shapes=[pltpu.SemaphoreType.DMA((nt * mine,))],
        compiler_params=params(16),
        input_output_aliases={1 + nt: 0} if given else {},
        cost_estimate=pl.CostEstimate(
            flops=0, bytes_accessed=4 * c * tokens * nt, transcendentals=0
        ),
    )(me, *slots, *given)


def swap(slots):
    n = len(slots)
    return [slots[0]] + [
        lax.ppermute(slots[s], "tensor", [(i, i ^ s) for i in range(n)]) for s in range(1, n)
    ]


def after(x, *deps):
    return pl.pallas_call(
        lambda *refs: None,
        in_specs=[ANY] * (1 + len(deps)),
        out_specs=ANY,
        out_shape=jax.ShapeDtypeStruct(x.shape, x.dtype),
        input_output_aliases={0: 0},
    )(x, *deps)


def flip(x, axis, n, bit):
    return lax.ppermute(x, axis, [(i, i ^ bit) for i in range(n)])


def gather_along(ns, both):
    got = [flip(both, "seq", ns, 2)]
    both = jnp.concatenate([both, got[0]])
    bit = 4
    if ns % 8 == 0:
        middle = [i for i in range(ns) if ((i >> 1) ^ (i >> 2)) & 1]
        got.append(lax.ppermute(both, "seq", [(i, i ^ 6) for i in middle]))
        got.append(lax.ppermute(got[1], "seq", [(i, i ^ 2) for i in middle]))
        both = jnp.concatenate([both, got[1] + got[2]])
        bit = 8
    while bit < ns:
        got.append(flip(both, "seq", ns, bit))
        both = jnp.concatenate([both, got[-1]])
        bit *= 2
    return both, got


def gather_across(nt, start, order):
    pieces = {0: start}
    for bit in order:
        pieces |= {s ^ bit: flip(x, "tensor", nt, bit) for s, x in pieces.items()}
    return pieces


def on_device(
    ns,
    nt,
    activations,
    first_factor,
    spectral,
    second_factor,
    gate_scale,
    gate_shift,
    expand_weight,
    reduce_weight,
):
    c = activations.shape[0]
    full = reduce_weight.shape[1]
    at = lax.axis_index("tensor")
    me = at.astype(jnp.int32).reshape(1)
    scale = lax.dynamic_slice_in_dim(gate_scale, at * c, c)[:, None]
    shift = lax.dynamic_slice_in_dim(gate_shift, at * c, c)[:, None]
    both, got = gather_along(ns, jnp.stack([expand_weight.T, reduce_weight])[None])
    bits = [1 << i for i in range(nt.bit_length() - 1)]
    near_in = gather_across(nt, both[:, 0].reshape(-1, full), bits)
    near_out = gather_across(nt, both[:, 1].reshape(-1, full).T, bits[::-1])
    halves_in = [jnp.stack([near_in[s] for s in range(nt)])]
    halves_in.append(flip(halves_in[0], "seq", ns, 1))
    halves_out = [jnp.stack([near_out[s] for s in range(nt)])]
    halves_out.append(flip(halves_out[0], "seq", ns, 1))

    def exchange(x):
        return lax.all_to_all(x, "seq", split_axis=0, concat_axis=0, tiled=True)

    def first(at, n, deps=()):
        return first_pass(at, n, activations, first_factor, spectral, ns, deps)

    def second(front, m, deps=(), groups=1):
        return second_pass(front, m, second_factor, groups, deps)

    def gated(k, back, deps=(), group=0):
        return gate(k, group, me, activations, back, scale, shift, nt, list(deps))

    def layer(slots, deps=()):
        return mlp(me, slots, halves_in, halves_out, list(deps))

    def put(k, done, result, group=0):
        return place(k, group, me, done, result, activations.shape)

    front01 = exchange(after(first(0, 2), got[0]))
    front23 = exchange(after(first(1, 2), got[1]))
    (mixed0,) = second(front01, 0, [near_in[bits[0]], near_out[bits[-1]]])
    (mixed1,) = second(front01, 1)
    back0 = exchange(mixed0)
    (mixed2,) = second(front23, 0, [halves_in[0], halves_out[0]])
    back1 = exchange(mixed1)
    mixed3 = second(front23, 1, [halves_in[1], halves_out[1]], 2)
    in0 = swap(gated(0, back0))
    out0 = layer(in0)
    back2 = exchange(after(mixed2, out0[0]))
    done0 = swap(out0)
    in1 = swap(gated(1, back1))
    out1 = layer(in1)
    back3a = exchange(after(mixed3[0], out1[0]))
    done1 = swap(out1)
    result = put(0, done0, None)
    in2 = swap(gated(2, back2, [result]))
    back3b = exchange(after(mixed3[1], *in2[1:]))
    gate3a = gated(3, back3a)
    in3a = swap(gate3a)
    out2 = layer(in2, [gate3a[0]])
    done2 = swap(out2)
    result = put(1, done1, result)
    gate3b = gated(3, back3b, [out2[0], result], 1)
    in3b = swap(gate3b)
    out3a = layer(in3a, [gate3b[0]])
    done3a = swap(out3a)
    result = put(2, done2, result)
    out3b = layer(in3b, [out3a[0], result])
    done3b = swap(out3b)
    result = put(3, done3a, result)
    return put(3, done3b, result, 1)


def solution(mesh):
    return jax.shard_map(
        functools.partial(on_device, mesh.shape["seq"], mesh.shape["tensor"]),
        mesh=mesh,
        in_specs=(
            P("tensor", "seq"),
            P(),
            P("tensor", "seq"),
            P(),
            P(),
            P(),
            P(None, ("seq", "tensor")),
            P(("seq", "tensor"), None),
        ),
        out_specs=P("tensor", "seq"),
        check_vma=False,
    )
```

```python
import functools

import jax
import jax.numpy as jnp
from jax import lax
from jax.experimental import pallas as pl
from jax.experimental.pallas import tpu as pltpu
from jax.sharding import PartitionSpec as P

B = 512
J = 128
epsilon = 1e-06
f32 = jnp.float32
bf16 = jnp.bfloat16
ANY = pl.BlockSpec(memory_space=pl.ANY)


def params(mib):
    return pltpu.CompilerParams(vmem_limit_bytes=mib * 2**20)


def first_pass(at, n, activations, first_factor, spectral, ns, deps=()):
    c, tokens = activations.shape
    blocks = tokens // B
    step = min(4, blocks)
    wide = n * J
    per = B // wide

    def kernel(act, factor, *rest):
        specs, out = rest[:step], rest[-1]
        for q in range(step):
            product = jnp.dot(act[:, q * B : (q + 1) * B], factor[...], preferred_element_type=f32)
            value = (product * specs[q][...]).astype(bf16)
            for m in range(n):
                out[:, m, q] = value[:, m * J : (m + 1) * J].reshape(ns, c // ns, J)

    def spec_at(q):
        return pl.BlockSpec((c, wide), lambda i: (0, (i * step + q) * per + at))

    return pl.pallas_call(
        kernel,
        grid=(blocks // step,),
        in_specs=[
            pl.BlockSpec((c, step * B), lambda i: (0, i)),
            pl.BlockSpec((B, wide), lambda i: (0, at)),
        ]
        + [spec_at(q) for q in range(step)]
        + [ANY] * len(deps),
        out_specs=pl.BlockSpec((ns, n, step, c // ns, J), lambda i: (0, 0, i, 0, 0)),
        out_shape=jax.ShapeDtypeStruct((ns, n, blocks, c // ns, J), bf16),
        compiler_params=params(32),
        cost_estimate=pl.CostEstimate(
            flops=2 * c * blocks * B * wide,
            bytes_accessed=2 * c * tokens + 6 * c * blocks * wide,
            transcendentals=0,
        ),
    )(activations, first_factor, *[spectral] * step, *deps)


def second_pass(gathered, m, second_factor, groups, deps=()):
    ns, _, blocks, c, _ = gathered.shape
    a = ns * blocks
    cb = min(16, c)
    part = blocks // groups

    def kernel(x_ref, s_ref, *rest):
        outs, (x_wide, y_wide) = rest[-groups - 2 : -2], rest[-2:]
        x_wide[...] = x_ref[...].astype(f32).reshape(a * cb, J)
        factor = s_ref[...]
        high = factor.astype(bf16)
        low = (factor - high.astype(f32)).astype(bf16)
        for i in range(0, cb, 2):
            x = jnp.concatenate(
                [x_wide[pl.ds(i + h, a, stride=cb), :] for h in range(2)], axis=1
            ).astype(bf16)
            y = jnp.dot(high, x, preferred_element_type=f32)
            y += jnp.dot(low, x, preferred_element_type=f32)
            for h in range(2):
                y_wide[pl.ds(i + h, a, stride=cb), :] = y[:, h * J : (h + 1) * J]
        y = y_wide[...].reshape(ns, blocks, cb, J)
        for g in range(groups):
            outs[g][...] = y[:, g * part : (g + 1) * part].astype(bf16)

    return pl.pallas_call(
        kernel,
        grid=(c // cb,),
        in_specs=[
            pl.BlockSpec((ns, 1, blocks, cb, J), lambda i: (0, m, 0, i, 0)),
            pl.BlockSpec((a, a), lambda i: (0, 0)),
        ]
        + [ANY] * len(deps),
        out_specs=[pl.BlockSpec((ns, part, cb, J), lambda i: (0, 0, i, 0))] * groups,
        out_shape=[jax.ShapeDtypeStruct((ns, part, c, J), bf16)] * groups,
        scratch_shapes=[pltpu.VMEM((a * cb, J), f32), pltpu.VMEM((a * cb, J), f32)],
        compiler_params=params(32),
        cost_estimate=pl.CostEstimate(
            flops=8 * a * a * c * J, bytes_accessed=4 * a * c * J, transcendentals=0
        ),
    )(gathered, second_factor, *deps)


def gate(k, group, me, activations, returned, scale, shift, nt, deps):
    c, tokens = activations.shape
    ns, blocks, ci, _ = returned.shape
    mine = blocks // nt
    step = min(2, mine)
    steps = mine // step
    begin = group * blocks // step

    def kernel(me_ref, *rest):
        acts, rets = rest[:nt], rest[nt : 2 * nt]
        scale_ref, shift_ref = rest[2 * nt : 2 * nt + 2]
        outs = rest[-nt:]
        for s in range(nt):
            for q in range(step):
                x = acts[s][:, q * B + k * J : q * B + (k + 1) * J].astype(f32)
                mixed = rets[s][:, q].reshape(c, J).astype(f32)
                gating = jax.nn.sigmoid(x * scale_ref[...] + shift_ref[...])
                outs[s][:, q * J : (q + 1) * J] = (x + gating * mixed).astype(bf16)

    def act_at(s):
        return pl.BlockSpec((c, step * B), lambda i, me: (0, begin + (me[0] ^ s) * steps + i))

    def ret_at(s):
        return pl.BlockSpec(
            (ns, step, ci, J), lambda i, me: (0, (me[0] ^ s) * steps + i, 0, 0)
        )

    column = pl.BlockSpec((c, 1), lambda i, me: (0, 0))
    return pl.pallas_call(
        kernel,
        grid_spec=pltpu.PrefetchScalarGridSpec(
            num_scalar_prefetch=1,
            grid=(steps,),
            in_specs=[act_at(s) for s in range(nt)]
            + [ret_at(s) for s in range(nt)]
            + [column, column]
            + [ANY] * len(deps),
            out_specs=[pl.BlockSpec((c, step * J), lambda i, me: (0, i))] * nt,
        ),
        out_shape=[jax.ShapeDtypeStruct((c, mine * J), bf16)] * nt,
        compiler_params=params(32),
        cost_estimate=pl.CostEstimate(
            flops=8 * c * blocks * J,
            bytes_accessed=2 * c * tokens + 4 * c * blocks * J,
            transcendentals=c * blocks * J,
        ),
    )(me, *[activations] * nt, *[returned] * nt, scale, shift, *deps)


def mlp(me, slots, halves_in, halves_out, deps):
    nt = len(slots)
    c, tokens = slots[0].shape
    half, hb, full = halves_in[0].shape
    n = 2 * half
    tile = min(256, tokens)

    def kernel(me_ref, *rest):
        xs, w1s, w2s = rest[:nt], rest[nt : nt + 2], rest[nt + 2 : nt + 4]
        outs = rest[-nt - 5 : -5]
        normed, total, w1, w2, sems = rest[-5:]
        step = pl.program_id(0)

        def fetch(piece, slot):
            return (
                pltpu.make_async_copy(
                    w1s[piece // half].at[piece % half], w1.at[slot], sems.at[0, slot]
                ),
                pltpu.make_async_copy(
                    w2s[piece // half].at[piece % half], w2.at[slot], sems.at[1, slot]
                ),
            )

        def start(piece):
            for copy in fetch(piece, piece % 2):
                copy.start()

        @pl.when(step == 0)
        def _():
            start(0)
            squares = jnp.zeros((1, tokens), f32)
            for s in range(nt):
                x = xs[s][...].astype(f32)
                squares += jnp.sum(x * x, axis=0, keepdims=True)
            scale = lax.rsqrt(squares / full + epsilon)
            for s in range(nt):
                at = pl.multiple_of((me_ref[0] ^ s) * c, c)
                normed[pl.ds(at, c), :] = (xs[s][...].astype(f32) * scale).astype(bf16)
            total[...] = jnp.zeros_like(total)

        for piece in range(1, n):
            pl.when(step == piece - 1)(functools.partial(start, piece))
        slot = lax.rem(step, 2)
        for copy in fetch(0, slot):
            copy.wait()

        def expand(t):
            return jnp.dot(w1[slot], normed[:, t : t + tile], preferred_element_type=f32)

        ahead = expand(0)
        for t in range(0, tokens, tile):
            x = ahead
            if t + tile < tokens:
                ahead = expand(t + tile)
            h = jax.nn.gelu(x).astype(bf16)
            total[:, t : t + tile] += jnp.dot(w2[slot], h, preferred_element_type=f32)

        @pl.when(step == n - 1)
        def _():
            for s in range(nt):
                at = pl.multiple_of((me_ref[0] ^ s) * c, c)
                outs[s][...] = (xs[s][...].astype(f32) + total[pl.ds(at, c), :]).astype(bf16)

    whole = pl.BlockSpec((c, tokens), lambda i, me: (0, 0))
    return pl.pallas_call(
        kernel,
        grid_spec=pltpu.PrefetchScalarGridSpec(
            num_scalar_prefetch=1,
            grid=(n,),
            in_specs=[whole] * nt + [ANY] * (4 + len(deps)),
            out_specs=[whole] * nt,
            scratch_shapes=[
                pltpu.VMEM((full, tokens), bf16),
                pltpu.VMEM((full, tokens), f32),
                pltpu.VMEM((2, hb, full), bf16),
                pltpu.VMEM((2, full, hb), bf16),
                pltpu.SemaphoreType.DMA((2, 2)),
            ],
        ),
        out_shape=[jax.ShapeDtypeStruct((c, tokens), bf16)] * nt,
        compiler_params=params(40),
        cost_estimate=pl.CostEstimate(
            flops=4 * full * hb * n * tokens,
            bytes_accessed=4 * full * hb * n + 4 * full * tokens,
            transcendentals=hb * n * tokens,
        ),
    )(me, *slots, *halves_in, *halves_out, *deps)


def place(k, group, me, slots, result, shape):
    nt = len(slots)
    c, tokens = slots[0].shape
    mine = tokens // J
    given = [] if result is None else [result]

    def kernel(me_ref, *rest):
        ys, out, sems = rest[:nt], rest[-2], rest[-1]
        copies = []
        for s in range(nt):
            for q in range(mine):
                block = group * nt * mine + (me_ref[0] ^ s) * mine + q
                at = pl.multiple_of(block * B + k * J, J)
                copies.append(
                    pltpu.make_async_copy(
                        ys[s].at[:, q * J : (q + 1) * J],
                        out.at[:, pl.ds(at, J)],
                        sems.at[s * mine + q],
                    )
                )
        for copy in copies:
            copy.start()
        for copy in copies:
            copy.wait()

    return pl.pallas_call(
        kernel,
        in_specs=[pl.BlockSpec(memory_space=pltpu.SMEM)]
        + [pl.BlockSpec(memory_space=pltpu.VMEM)] * nt
        + [ANY] * len(given),
        out_specs=ANY,
        out_shape=jax.ShapeDtypeStruct(shape, bf16),
        scratch_shapes=[pltpu.SemaphoreType.DMA((nt * mine,))],
        compiler_params=params(16),
        input_output_aliases={1 + nt: 0} if given else {},
        cost_estimate=pl.CostEstimate(
            flops=0, bytes_accessed=4 * c * tokens * nt, transcendentals=0
        ),
    )(me, *slots, *given)


def swap(slots):
    n = len(slots)
    return [slots[0]] + [
        lax.ppermute(slots[s], "tensor", [(i, i ^ s) for i in range(n)]) for s in range(1, n)
    ]


def after(x, *deps):
    return pl.pallas_call(
        lambda *refs: None,
        in_specs=[ANY] * (1 + len(deps)),
        out_specs=ANY,
        out_shape=jax.ShapeDtypeStruct(x.shape, x.dtype),
        input_output_aliases={0: 0},
    )(x, *deps)


def flip(x, axis, n, bit):
    return lax.ppermute(x, axis, [(i, i ^ bit) for i in range(n)])


def gather_along(ns, both):
    got = [flip(both, "seq", ns, 2)]
    both = jnp.concatenate([both, got[0]])
    bit = 4
    if ns % 8 == 0:
        middle = [i for i in range(ns) if ((i >> 1) ^ (i >> 2)) & 1]
        got.append(lax.ppermute(both, "seq", [(i, i ^ 6) for i in middle]))
        got.append(lax.ppermute(got[1], "seq", [(i, i ^ 2) for i in middle]))
        both = jnp.concatenate([both, got[1] + got[2]])
        bit = 8
    while bit < ns:
        got.append(flip(both, "seq", ns, bit))
        both = jnp.concatenate([both, got[-1]])
        bit *= 2
    return both, got


def gather_across(nt, start, order):
    pieces = {0: start}
    for bit in order:
        pieces |= {s ^ bit: flip(x, "tensor", nt, bit) for s, x in pieces.items()}
    return pieces


def on_device(
    ns,
    nt,
    activations,
    first_factor,
    spectral,
    second_factor,
    gate_scale,
    gate_shift,
    expand_weight,
    reduce_weight,
):
    c = activations.shape[0]
    full = reduce_weight.shape[1]
    at = lax.axis_index("tensor")
    me = at.astype(jnp.int32).reshape(1)
    scale = lax.dynamic_slice_in_dim(gate_scale, at * c, c)[:, None]
    shift = lax.dynamic_slice_in_dim(gate_shift, at * c, c)[:, None]
    both, got = gather_along(ns, jnp.stack([expand_weight.T, reduce_weight])[None])
    bits = [1 << i for i in range(nt.bit_length() - 1)]
    near_in = gather_across(nt, both[:, 0].reshape(-1, full), bits)
    near_out = gather_across(nt, both[:, 1].reshape(-1, full).T, bits[::-1])
    halves_in = [jnp.stack([near_in[s] for s in range(nt)])]
    halves_in.append(flip(halves_in[0], "seq", ns, 1))
    halves_out = [jnp.stack([near_out[s] for s in range(nt)])]
    halves_out.append(flip(halves_out[0], "seq", ns, 1))

    def exchange(x):
        return lax.all_to_all(x, "seq", split_axis=0, concat_axis=0, tiled=True)

    def first(at, n, deps=()):
        return first_pass(at, n, activations, first_factor, spectral, ns, deps)

    def second(front, m, deps=(), groups=1):
        return second_pass(front, m, second_factor, groups, deps)

    def gated(k, back, deps=(), group=0):
        return gate(k, group, me, activations, back, scale, shift, nt, list(deps))

    def layer(slots, deps=()):
        return mlp(me, slots, halves_in, halves_out, list(deps))

    def put(k, done, result, group=0):
        return place(k, group, me, done, result, activations.shape)

    front01 = exchange(after(first(0, 2), got[1]))
    front23 = exchange(after(first(1, 2), got[-1]))
    (mixed0,) = second(front01, 0, [near_in[bits[0]], near_out[bits[-1]]])
    (mixed1,) = second(front01, 1)
    back0 = exchange(mixed0)
    (mixed2,) = second(front23, 0, [halves_in[0], halves_out[0]])
    back1 = exchange(mixed1)
    (mixed3,) = second(front23, 1, [halves_in[1], halves_out[1]])
    in0 = swap(gated(0, back0))
    back2 = exchange(after(mixed2, *in0[1:]))
    gate1 = gated(1, back1)
    in1 = swap(gate1)
    out0 = layer(in0, [gate1[0]])
    back3 = exchange(after(mixed3, out0[0], *in1[1:]))
    done0 = swap(out0)
    gate2 = gated(2, back2)
    in2 = swap(gate2)
    out1 = layer(in1, [gate2[0]])
    done1 = swap(out1)
    result = put(0, done0, None)
    gate3 = gated(3, back3, [out1[0], in2[1], result])
    in3 = swap(gate3)
    out2 = layer(in2, [gate3[0]])
    done2 = swap(out2)
    result = put(1, done1, result)
    out3 = layer(in3, [out2[0], result])
    done3 = swap(out3)
    result = put(2, done2, result)
    return put(3, done3, result)


def solution(mesh):
    return jax.shard_map(
        functools.partial(on_device, mesh.shape["seq"], mesh.shape["tensor"]),
        mesh=mesh,
        in_specs=(
            P("tensor", "seq"),
            P(),
            P("tensor", "seq"),
            P(),
            P(),
            P(),
            P(None, ("seq", "tensor")),
            P(("seq", "tensor"), None),
        ),
        out_specs=P("tensor", "seq"),
        check_vma=False,
    )
```

```python
import functools
import math

import jax
import jax.numpy as jnp
from jax import lax
from jax.experimental import pallas as pl
from jax.experimental.pallas import tpu as pltpu
from jax.sharding import PartitionSpec as P

B = 512
J = 128
epsilon = 1e-06
inside = (2 / math.pi) ** 0.5
cubic = 0.044715 * inside
f32 = jnp.float32
bf16 = jnp.bfloat16
ANY = pl.BlockSpec(memory_space=pl.ANY)


def params(mib):
    return pltpu.CompilerParams(vmem_limit_bytes=mib * 2**20)


def first_pass(at, n, activations, first_factor, spectral, ns, deps=()):
    c, tokens = activations.shape
    blocks = tokens // B
    step = min(4, blocks)
    wide = n * J
    per = B // wide

    def kernel(act, factor, *rest):
        specs, out = rest[:step], rest[-1]
        for q in range(step):
            product = jnp.dot(act[:, q * B : (q + 1) * B], factor[...], preferred_element_type=f32)
            value = (product * specs[q][...]).astype(bf16)
            for m in range(n):
                out[:, m, q] = value[:, m * J : (m + 1) * J].reshape(ns, c // ns, J)

    def spec_at(q):
        return pl.BlockSpec((c, wide), lambda i: (0, (i * step + q) * per + at))

    return pl.pallas_call(
        kernel,
        grid=(blocks // step,),
        in_specs=[
            pl.BlockSpec((c, step * B), lambda i: (0, i)),
            pl.BlockSpec((B, wide), lambda i: (0, at)),
        ]
        + [spec_at(q) for q in range(step)]
        + [ANY] * len(deps),
        out_specs=pl.BlockSpec((ns, n, step, c // ns, J), lambda i: (0, 0, i, 0, 0)),
        out_shape=jax.ShapeDtypeStruct((ns, n, blocks, c // ns, J), bf16),
        compiler_params=params(32),
        cost_estimate=pl.CostEstimate(
            flops=2 * c * blocks * B * wide,
            bytes_accessed=2 * c * tokens + 6 * c * blocks * wide,
            transcendentals=0,
        ),
    )(activations, first_factor, *[spectral] * step, *deps)


def second_pass(gathered, m, second_factor, groups, deps=()):
    ns, _, blocks, c, _ = gathered.shape
    a = ns * blocks
    cb = min(16, c)
    part = blocks // groups

    def kernel(x_ref, s_ref, *rest):
        outs, (x_wide, y_wide) = rest[-groups - 2 : -2], rest[-2:]
        x_wide[...] = x_ref[...].astype(f32).reshape(a * cb, J)
        factor = s_ref[...]
        high = factor.astype(bf16)
        low = (factor - high.astype(f32)).astype(bf16)
        for i in range(0, cb, 2):
            x = jnp.concatenate(
                [x_wide[pl.ds(i + h, a, stride=cb), :] for h in range(2)], axis=1
            ).astype(bf16)
            y = jnp.dot(high, x, preferred_element_type=f32)
            y += jnp.dot(low, x, preferred_element_type=f32)
            for h in range(2):
                y_wide[pl.ds(i + h, a, stride=cb), :] = y[:, h * J : (h + 1) * J]
        y = y_wide[...].reshape(ns, blocks, cb, J)
        for g in range(groups):
            outs[g][...] = y[:, g * part : (g + 1) * part].astype(bf16)

    return pl.pallas_call(
        kernel,
        grid=(c // cb,),
        in_specs=[
            pl.BlockSpec((ns, 1, blocks, cb, J), lambda i: (0, m, 0, i, 0)),
            pl.BlockSpec((a, a), lambda i: (0, 0)),
        ]
        + [ANY] * len(deps),
        out_specs=[pl.BlockSpec((ns, part, cb, J), lambda i: (0, 0, i, 0))] * groups,
        out_shape=[jax.ShapeDtypeStruct((ns, part, c, J), bf16)] * groups,
        scratch_shapes=[pltpu.VMEM((a * cb, J), f32), pltpu.VMEM((a * cb, J), f32)],
        compiler_params=params(32),
        cost_estimate=pl.CostEstimate(
            flops=8 * a * a * c * J, bytes_accessed=4 * a * c * J, transcendentals=0
        ),
    )(gathered, second_factor, *deps)


def gate(k, group, me, activations, returned, scale, shift, nt, deps):
    c, tokens = activations.shape
    ns, blocks, ci, _ = returned.shape
    mine = blocks // nt
    step = min(2, mine)
    steps = mine // step
    begin = group * blocks // step

    def kernel(me_ref, *rest):
        acts, rets = rest[:nt], rest[nt : 2 * nt]
        scale_ref, shift_ref = rest[2 * nt : 2 * nt + 2]
        outs = rest[-nt:]
        for s in range(nt):
            for q in range(step):
                x = acts[s][:, q * B + k * J : q * B + (k + 1) * J].astype(f32)
                mixed = rets[s][:, q].reshape(c, J).astype(f32)
                gating = jax.nn.sigmoid(x * scale_ref[...] + shift_ref[...])
                outs[s][:, q * J : (q + 1) * J] = (x + gating * mixed).astype(bf16)

    def act_at(s):
        return pl.BlockSpec((c, step * B), lambda i, me: (0, begin + (me[0] ^ s) * steps + i))

    def ret_at(s):
        return pl.BlockSpec(
            (ns, step, ci, J), lambda i, me: (0, (me[0] ^ s) * steps + i, 0, 0)
        )

    column = pl.BlockSpec((c, 1), lambda i, me: (0, 0))
    return pl.pallas_call(
        kernel,
        grid_spec=pltpu.PrefetchScalarGridSpec(
            num_scalar_prefetch=1,
            grid=(steps,),
            in_specs=[act_at(s) for s in range(nt)]
            + [ret_at(s) for s in range(nt)]
            + [column, column]
            + [ANY] * len(deps),
            out_specs=[pl.BlockSpec((c, step * J), lambda i, me: (0, i))] * nt,
        ),
        out_shape=[jax.ShapeDtypeStruct((c, mine * J), bf16)] * nt,
        compiler_params=params(56),
        cost_estimate=pl.CostEstimate(
            flops=8 * c * blocks * J,
            bytes_accessed=2 * c * tokens + 4 * c * blocks * J,
            transcendentals=c * blocks * J,
        ),
    )(me, *[activations] * nt, *[returned] * nt, scale, shift, *deps)


def mlp(me, slots, halves_in, halves_out, deps):
    nt = len(slots)
    c, tokens = slots[0].shape
    half, hb, full = halves_in[0].shape
    n = 2 * half
    tile = min(256, tokens)

    def kernel(me_ref, *rest):
        xs, w1s, w2s = rest[:nt], rest[nt : nt + 2], rest[nt + 2 : nt + 4]
        outs = rest[-nt - 5 : -5]
        normed, total, w1, w2, sems = rest[-5:]
        step = pl.program_id(0)

        def fetch(piece, slot):
            return (
                pltpu.make_async_copy(
                    w1s[piece // half].at[piece % half], w1.at[slot], sems.at[0, slot]
                ),
                pltpu.make_async_copy(
                    w2s[piece // half].at[piece % half], w2.at[slot], sems.at[1, slot]
                ),
            )

        def start(piece):
            for copy in fetch(piece, piece % 2):
                copy.start()

        @pl.when(step == 0)
        def _():
            start(0)
            squares = jnp.zeros((1, tokens), f32)
            for s in range(nt):
                x = xs[s][...].astype(f32)
                squares += jnp.sum(x * x, axis=0, keepdims=True)
            scale = lax.rsqrt(squares / full + epsilon)
            for s in range(nt):
                at = pl.multiple_of((me_ref[0] ^ s) * c, c)
                normed[pl.ds(at, c), :] = (xs[s][...].astype(f32) * scale).astype(bf16)
            total[...] = jnp.zeros_like(total)

        for piece in range(1, n):
            pl.when(step == piece - 1)(functools.partial(start, piece))
        slot = lax.rem(step, 2)
        for copy in fetch(0, slot):
            copy.wait()

        def expand(t):
            return jnp.dot(w1[slot], normed[:, t : t + tile], preferred_element_type=f32)

        ahead = expand(0)
        for t in range(0, tokens, tile):
            x = ahead
            if t + tile < tokens:
                ahead = expand(t + tile)
            h = (x + x * jnp.tanh(x * (inside + cubic * (x * x)))).astype(bf16)
            total[:, t : t + tile] += jnp.dot(w2[slot], h, preferred_element_type=f32)

        @pl.when(step == n - 1)
        def _():
            for s in range(nt):
                at = pl.multiple_of((me_ref[0] ^ s) * c, c)
                outs[s][...] = (xs[s][...].astype(f32) + 0.5 * total[pl.ds(at, c), :]).astype(bf16)

    whole = pl.BlockSpec((c, tokens), lambda i, me: (0, 0))
    return pl.pallas_call(
        kernel,
        grid_spec=pltpu.PrefetchScalarGridSpec(
            num_scalar_prefetch=1,
            grid=(n,),
            in_specs=[whole] * nt + [ANY] * (4 + len(deps)),
            out_specs=[whole] * nt,
            scratch_shapes=[
                pltpu.VMEM((full, tokens), bf16),
                pltpu.VMEM((full, tokens), f32),
                pltpu.VMEM((2, hb, full), bf16),
                pltpu.VMEM((2, full, hb), bf16),
                pltpu.SemaphoreType.DMA((2, 2)),
            ],
        ),
        out_shape=[jax.ShapeDtypeStruct((c, tokens), bf16)] * nt,
        compiler_params=params(56),
        cost_estimate=pl.CostEstimate(
            flops=4 * full * hb * n * tokens,
            bytes_accessed=4 * full * hb * n + 4 * full * tokens,
            transcendentals=hb * n * tokens,
        ),
    )(me, *slots, *halves_in, *halves_out, *deps)


def place(k, group, me, slots, result, shape):
    nt = len(slots)
    c, tokens = slots[0].shape
    mine = tokens // J
    given = [] if result is None else [result]

    def kernel(me_ref, *rest):
        ys, out, sems = rest[:nt], rest[-2], rest[-1]
        copies = []
        for s in range(nt):
            for q in range(mine):
                block = group * nt * mine + (me_ref[0] ^ s) * mine + q
                at = pl.multiple_of(block * B + k * J, J)
                copies.append(
                    pltpu.make_async_copy(
                        ys[s].at[:, q * J : (q + 1) * J],
                        out.at[:, pl.ds(at, J)],
                        sems.at[s * mine + q],
                    )
                )
        for copy in copies:
            copy.start()
        for copy in copies:
            copy.wait()

    return pl.pallas_call(
        kernel,
        in_specs=[pl.BlockSpec(memory_space=pltpu.SMEM)]
        + [pl.BlockSpec(memory_space=pltpu.VMEM)] * nt
        + [ANY] * len(given),
        out_specs=ANY,
        out_shape=jax.ShapeDtypeStruct(shape, bf16),
        scratch_shapes=[pltpu.SemaphoreType.DMA((nt * mine,))],
        compiler_params=params(16),
        input_output_aliases={1 + nt: 0} if given else {},
        cost_estimate=pl.CostEstimate(
            flops=0, bytes_accessed=4 * c * tokens * nt, transcendentals=0
        ),
    )(me, *slots, *given)


def swap(slots):
    n = len(slots)
    return [slots[0]] + [
        lax.ppermute(slots[s], "tensor", [(i, i ^ s) for i in range(n)]) for s in range(1, n)
    ]


def after(x, *deps):
    return pl.pallas_call(
        lambda *refs: None,
        in_specs=[ANY] * (1 + len(deps)),
        out_specs=ANY,
        out_shape=jax.ShapeDtypeStruct(x.shape, x.dtype),
        input_output_aliases={0: 0},
    )(x, *deps)


def flip(x, axis, n, bit):
    return lax.ppermute(x, axis, [(i, i ^ bit) for i in range(n)])


def gather_along(ns, both):
    if ns % 8:
        bit, marks = 2, [both, both]
    else:
        middle = [i for i in range(ns) if ((i >> 1) ^ (i >> 2)) & 1]
        across = [(i, i ^ 6) for i in middle]
        inner = lax.ppermute(both, "seq", across)
        outer = lax.ppermute(both, "seq", [(i ^ 2, i) for i in middle])
        beyond = lax.ppermute(outer, "seq", across)
        out = lax.ppermute(
            jnp.concatenate([both, inner, beyond]), "seq", [(i, i ^ 2) for i in middle]
        )
        both = jnp.concatenate([both, jnp.concatenate([outer, inner, beyond]) + out])
        bit, marks = 8, [beyond, out]
    while bit < ns:
        marks[1] = flip(both, "seq", ns, bit)
        both = jnp.concatenate([both, marks[1]])
        bit *= 2
    return both, marks


def gather_across(nt, start, order):
    pieces = {0: start}
    for bit in order:
        pieces |= {s ^ bit: flip(x, "tensor", nt, bit) for s, x in pieces.items()}
    return pieces


def on_device(
    ns,
    nt,
    activations,
    first_factor,
    spectral,
    second_factor,
    gate_scale,
    gate_shift,
    expand_weight,
    reduce_weight,
):
    c = activations.shape[0]
    full = reduce_weight.shape[1]
    at = lax.axis_index("tensor")
    me = at.astype(jnp.int32).reshape(1)
    scale = lax.dynamic_slice_in_dim(gate_scale, at * c, c)[:, None]
    shift = lax.dynamic_slice_in_dim(gate_shift, at * c, c)[:, None]
    both, got = gather_along(ns, jnp.stack([expand_weight.T, reduce_weight])[None])
    bits = [1 << i for i in range(nt.bit_length() - 1)]
    near_in = gather_across(nt, both[:, 0].reshape(-1, full), bits)
    near_out = gather_across(nt, both[:, 1].reshape(-1, full).T, bits[::-1])
    halves_in = [jnp.stack([near_in[s] for s in range(nt)])]
    halves_in.append(flip(halves_in[0], "seq", ns, 1))
    halves_out = [jnp.stack([near_out[s] for s in range(nt)])]
    halves_out.append(flip(halves_out[0], "seq", ns, 1))

    def exchange(x):
        return lax.all_to_all(x, "seq", split_axis=0, concat_axis=0, tiled=True)

    def first(at, n, deps=()):
        return first_pass(at, n, activations, first_factor, spectral, ns, deps)

    def second(front, m, deps=(), groups=1):
        return second_pass(front, m, second_factor, groups, deps)

    def gated(k, back, deps=(), group=0):
        return gate(k, group, me, activations, back, scale, shift, nt, list(deps))

    def layer(slots, deps=()):
        return mlp(me, slots, halves_in, halves_out, list(deps))

    def put(k, done, result, group=0):
        return place(k, group, me, done, result, activations.shape)

    front01 = exchange(after(first(0, 2), got[0]))
    front23 = exchange(after(first(1, 2), got[1]))
    (mixed0,) = second(front01, 0, [near_in[bits[0]], near_out[bits[-1]]])
    (mixed1,) = second(front01, 1)
    back0 = exchange(mixed0)
    (mixed2,) = second(front23, 0, [halves_in[0], halves_out[0]])
    back1 = exchange(mixed1)
    (mixed3,) = second(front23, 1, [halves_in[1], halves_out[1]])
    in0 = swap(gated(0, back0))
    back2 = exchange(after(mixed2, *in0[1:]))
    gate1 = gated(1, back1)
    in1 = swap(gate1)
    out0 = layer(in0, [gate1[0]])
    back3 = exchange(after(mixed3, out0[0], *in1[1:]))
    done0 = swap(out0)
    gate2 = gated(2, back2)
    in2 = swap(gate2)
    out1 = layer(in1, [gate2[0]])
    done1 = swap(out1)
    result = put(0, done0, None)
    gate3 = gated(3, back3, [out1[0], in2[1]])
    in3 = swap(gate3)
    out2 = layer(in2, [gate3[0], result])
    done2 = swap(out2)
    result = put(1, done1, result)
    out3 = layer(in3, [out2[0], result])
    done3 = swap(out3)
    result = put(2, done2, result)
    return put(3, done3, result)


def solution(mesh):
    return jax.shard_map(
        functools.partial(on_device, mesh.shape["seq"], mesh.shape["tensor"]),
        mesh=mesh,
        in_specs=(
            P("tensor", "seq"),
            P(),
            P("tensor", "seq"),
            P(),
            P(),
            P(),
            P(None, ("seq", "tensor")),
            P(("seq", "tensor"), None),
        ),
        out_specs=P("tensor", "seq"),
        check_vma=False,
    )
```

```python
import functools
import math

import jax
import jax.numpy as jnp
from jax import lax
from jax.experimental import pallas as pl
from jax.experimental.pallas import tpu as pltpu
from jax.sharding import PartitionSpec as P

B = 512
J = 128
epsilon = 1e-06
inside = (2 / math.pi) ** 0.5
cubic = 0.044715 * inside
f32 = jnp.float32
bf16 = jnp.bfloat16
ANY = pl.BlockSpec(memory_space=pl.ANY)


def params(mib):
    return pltpu.CompilerParams(vmem_limit_bytes=mib * 2**20)


def first_pass(at, n, activations, first_factor, spectral, ns, deps=()):
    c, tokens = activations.shape
    blocks = tokens // B
    step = min(4, blocks)
    wide = n * J
    per = B // wide

    def kernel(act, factor, *rest):
        specs, out = rest[:step], rest[-1]
        for q in range(step):
            product = jnp.dot(act[:, q * B : (q + 1) * B], factor[...], preferred_element_type=f32)
            value = (product * specs[q][...]).astype(bf16)
            for m in range(n):
                out[:, m, q] = value[:, m * J : (m + 1) * J].reshape(ns, c // ns, J)

    def spec_at(q):
        return pl.BlockSpec((c, wide), lambda i: (0, (i * step + q) * per + at))

    return pl.pallas_call(
        kernel,
        grid=(blocks // step,),
        in_specs=[
            pl.BlockSpec((c, step * B), lambda i: (0, i)),
            pl.BlockSpec((B, wide), lambda i: (0, at)),
        ]
        + [spec_at(q) for q in range(step)]
        + [ANY] * len(deps),
        out_specs=pl.BlockSpec((ns, n, step, c // ns, J), lambda i: (0, 0, i, 0, 0)),
        out_shape=jax.ShapeDtypeStruct((ns, n, blocks, c // ns, J), bf16),
        compiler_params=params(32),
        cost_estimate=pl.CostEstimate(
            flops=2 * c * blocks * B * wide,
            bytes_accessed=2 * c * tokens + 6 * c * blocks * wide,
            transcendentals=0,
        ),
    )(activations, first_factor, *[spectral] * step, *deps)


def second_pass(gathered, m, second_factor, groups, deps=()):
    ns, _, blocks, c, _ = gathered.shape
    a = ns * blocks
    cb = min(16, c)
    part = blocks // groups

    def kernel(x_ref, s_ref, *rest):
        outs, (x_wide, y_wide) = rest[-groups - 2 : -2], rest[-2:]
        x_wide[...] = x_ref[...].astype(f32).reshape(a * cb, J)
        factor = s_ref[...]
        high = factor.astype(bf16)
        low = (factor - high.astype(f32)).astype(bf16)
        for i in range(0, cb, 2):
            x = jnp.concatenate(
                [x_wide[pl.ds(i + h, a, stride=cb), :] for h in range(2)], axis=1
            ).astype(bf16)
            y = jnp.dot(high, x, preferred_element_type=f32)
            y += jnp.dot(low, x, preferred_element_type=f32)
            for h in range(2):
                y_wide[pl.ds(i + h, a, stride=cb), :] = y[:, h * J : (h + 1) * J]
        y = y_wide[...].reshape(ns, blocks, cb, J)
        for g in range(groups):
            outs[g][...] = y[:, g * part : (g + 1) * part].astype(bf16)

    return pl.pallas_call(
        kernel,
        grid=(c // cb,),
        in_specs=[
            pl.BlockSpec((ns, 1, blocks, cb, J), lambda i: (0, m, 0, i, 0)),
            pl.BlockSpec((a, a), lambda i: (0, 0)),
        ]
        + [ANY] * len(deps),
        out_specs=[pl.BlockSpec((ns, part, cb, J), lambda i: (0, 0, i, 0))] * groups,
        out_shape=[jax.ShapeDtypeStruct((ns, part, c, J), bf16)] * groups,
        scratch_shapes=[pltpu.VMEM((a * cb, J), f32), pltpu.VMEM((a * cb, J), f32)],
        compiler_params=params(32),
        cost_estimate=pl.CostEstimate(
            flops=8 * a * a * c * J, bytes_accessed=4 * a * c * J, transcendentals=0
        ),
    )(gathered, second_factor, *deps)


def gate(k, group, me, activations, returned, scale, shift, nt, deps):
    c, tokens = activations.shape
    ns, blocks, ci, _ = returned.shape
    mine = blocks // nt
    step = min(2, mine)
    steps = mine // step
    begin = group * blocks // step

    def kernel(me_ref, *rest):
        acts, rets = rest[:nt], rest[nt : 2 * nt]
        scale_ref, shift_ref = rest[2 * nt : 2 * nt + 2]
        outs = rest[-nt:]
        for s in range(nt):
            for q in range(step):
                x = acts[s][:, q * B + k * J : q * B + (k + 1) * J].astype(f32)
                mixed = rets[s][:, q].reshape(c, J).astype(f32)
                gating = jax.nn.sigmoid(x * scale_ref[...] + shift_ref[...])
                outs[s][:, q * J : (q + 1) * J] = (x + gating * mixed).astype(bf16)

    def act_at(s):
        return pl.BlockSpec((c, step * B), lambda i, me: (0, begin + (me[0] ^ s) * steps + i))

    def ret_at(s):
        return pl.BlockSpec(
            (ns, step, ci, J), lambda i, me: (0, (me[0] ^ s) * steps + i, 0, 0)
        )

    column = pl.BlockSpec((c, 1), lambda i, me: (0, 0))
    return pl.pallas_call(
        kernel,
        grid_spec=pltpu.PrefetchScalarGridSpec(
            num_scalar_prefetch=1,
            grid=(steps,),
            in_specs=[act_at(s) for s in range(nt)]
            + [ret_at(s) for s in range(nt)]
            + [column, column]
            + [ANY] * len(deps),
            out_specs=[pl.BlockSpec((c, step * J), lambda i, me: (0, i))] * nt,
        ),
        out_shape=[jax.ShapeDtypeStruct((c, mine * J), bf16)] * nt,
        compiler_params=params(56),
        cost_estimate=pl.CostEstimate(
            flops=8 * c * blocks * J,
            bytes_accessed=2 * c * tokens + 4 * c * blocks * J,
            transcendentals=c * blocks * J,
        ),
    )(me, *[activations] * nt, *[returned] * nt, scale, shift, *deps)


def mlp(me, slots, halves_in, halves_out, deps):
    nt = len(slots)
    c, tokens = slots[0].shape
    half, hb, full = halves_in[0].shape
    n = 2 * half
    tile = min(256, tokens)

    def kernel(me_ref, *rest):
        xs, w1s, w2s = rest[:nt], rest[nt : nt + 2], rest[nt + 2 : nt + 4]
        outs = rest[-nt - 5 : -5]
        normed, total, w1, w2, sems = rest[-5:]
        step = pl.program_id(0)

        def fetch(pair, slot):
            copies = []
            for h in range(2):
                which, at = divmod(2 * pair + h, half)
                rows = slice(h * hb, (h + 1) * hb)
                copies += [
                    pltpu.make_async_copy(
                        w1s[which].at[at], w1.at[slot, rows], sems.at[0, h, slot]
                    ),
                    pltpu.make_async_copy(
                        w2s[which].at[at], w2.at[slot, :, rows], sems.at[1, h, slot]
                    ),
                ]
            return copies

        def start(pair):
            for copy in fetch(pair, pair % 2):
                copy.start()

        @pl.when(step == 0)
        def _():
            start(0)
            squares = jnp.zeros((1, tokens), f32)
            for s in range(nt):
                x = xs[s][...].astype(f32)
                squares += jnp.sum(x * x, axis=0, keepdims=True)
            scale = lax.rsqrt(squares / full + epsilon)
            for s in range(nt):
                at = pl.multiple_of((me_ref[0] ^ s) * c, c)
                normed[pl.ds(at, c), :] = (xs[s][...].astype(f32) * scale).astype(bf16)
            total[...] = jnp.zeros_like(total)

        for pair in range(1, half):
            pl.when(step == pair - 1)(functools.partial(start, pair))
        slot = lax.rem(step, 2)
        for copy in fetch(0, slot):
            copy.wait()

        def expand(t):
            return jnp.dot(w1[slot], normed[:, t : t + tile], preferred_element_type=f32)

        ahead = expand(0)
        for t in range(0, tokens, tile):
            x = ahead
            if t + tile < tokens:
                ahead = expand(t + tile)
            h = (x + x * jnp.tanh(x * (inside + cubic * (x * x)))).astype(bf16)
            total[:, t : t + tile] += jnp.dot(w2[slot], h, preferred_element_type=f32)

        @pl.when(step == half - 1)
        def _():
            for s in range(nt):
                at = pl.multiple_of((me_ref[0] ^ s) * c, c)
                outs[s][...] = (xs[s][...].astype(f32) + 0.5 * total[pl.ds(at, c), :]).astype(bf16)

    whole = pl.BlockSpec((c, tokens), lambda i, me: (0, 0))
    return pl.pallas_call(
        kernel,
        grid_spec=pltpu.PrefetchScalarGridSpec(
            num_scalar_prefetch=1,
            grid=(half,),
            in_specs=[whole] * nt + [ANY] * (4 + len(deps)),
            out_specs=[whole] * nt,
            scratch_shapes=[
                pltpu.VMEM((full, tokens), bf16),
                pltpu.VMEM((full, tokens), f32),
                pltpu.VMEM((2, 2 * hb, full), bf16),
                pltpu.VMEM((2, full, 2 * hb), bf16),
                pltpu.SemaphoreType.DMA((2, 2, 2)),
            ],
        ),
        out_shape=[jax.ShapeDtypeStruct((c, tokens), bf16)] * nt,
        compiler_params=params(44),
        cost_estimate=pl.CostEstimate(
            flops=4 * full * hb * n * tokens,
            bytes_accessed=4 * full * hb * n + 4 * full * tokens,
            transcendentals=hb * n * tokens,
        ),
    )(me, *slots, *halves_in, *halves_out, *deps)


def place(k, group, me, slots, result, shape):
    nt = len(slots)
    c, tokens = slots[0].shape
    mine = tokens // J
    given = [] if result is None else [result]

    def kernel(me_ref, *rest):
        ys, out, sems = rest[:nt], rest[-2], rest[-1]
        copies = []
        for s in range(nt):
            for q in range(mine):
                block = group * nt * mine + (me_ref[0] ^ s) * mine + q
                at = pl.multiple_of(block * B + k * J, J)
                copies.append(
                    pltpu.make_async_copy(
                        ys[s].at[:, q * J : (q + 1) * J],
                        out.at[:, pl.ds(at, J)],
                        sems.at[s * mine + q],
                    )
                )
        for copy in copies:
            copy.start()
        for copy in copies:
            copy.wait()

    return pl.pallas_call(
        kernel,
        in_specs=[pl.BlockSpec(memory_space=pltpu.SMEM)]
        + [pl.BlockSpec(memory_space=pltpu.VMEM)] * nt
        + [ANY] * len(given),
        out_specs=ANY,
        out_shape=jax.ShapeDtypeStruct(shape, bf16),
        scratch_shapes=[pltpu.SemaphoreType.DMA((nt * mine,))],
        compiler_params=params(16),
        input_output_aliases={1 + nt: 0} if given else {},
        cost_estimate=pl.CostEstimate(
            flops=0, bytes_accessed=4 * c * tokens * nt, transcendentals=0
        ),
    )(me, *slots, *given)


def swap(slots):
    n = len(slots)
    return [slots[0]] + [
        lax.ppermute(slots[s], "tensor", [(i, i ^ s) for i in range(n)]) for s in range(1, n)
    ]


def after(x, *deps):
    return pl.pallas_call(
        lambda *refs: None,
        in_specs=[ANY] * (1 + len(deps)),
        out_specs=ANY,
        out_shape=jax.ShapeDtypeStruct(x.shape, x.dtype),
        input_output_aliases={0: 0},
    )(x, *deps)


def flip(x, axis, n, bit):
    return lax.ppermute(x, axis, [(i, i ^ bit) for i in range(n)])


def gather_along(ns, both):
    if ns % 8:
        bit, marks = 2, [both, both, both]
    else:
        middle = [i for i in range(ns) if ((i >> 1) ^ (i >> 2)) & 1]
        across = [(i, i ^ 6) for i in middle]
        inner = lax.ppermute(both, "seq", across)
        outer = lax.ppermute(both, "seq", [(i ^ 2, i) for i in middle])
        beyond = lax.ppermute(outer, "seq", across)
        out = lax.ppermute(
            jnp.concatenate([both, inner, beyond]), "seq", [(i, i ^ 2) for i in middle]
        )
        both = jnp.concatenate([both, jnp.concatenate([outer, inner, beyond]) + out])
        bit, marks = 8, [beyond, out, inner]
    while bit < ns:
        marks[1] = flip(both, "seq", ns, bit)
        both = jnp.concatenate([both, marks[1]])
        bit *= 2
    return both, marks


def gather_across(nt, start, order):
    pieces = {0: start}
    for bit in order:
        pieces |= {s ^ bit: flip(x, "tensor", nt, bit) for s, x in pieces.items()}
    return pieces


def on_device(
    ns,
    nt,
    activations,
    first_factor,
    spectral,
    second_factor,
    gate_scale,
    gate_shift,
    expand_weight,
    reduce_weight,
):
    c = activations.shape[0]
    full = reduce_weight.shape[1]
    at = lax.axis_index("tensor")
    me = at.astype(jnp.int32).reshape(1)
    scale = lax.dynamic_slice_in_dim(gate_scale, at * c, c)[:, None]
    shift = lax.dynamic_slice_in_dim(gate_shift, at * c, c)[:, None]
    both, got = gather_along(ns, jnp.stack([expand_weight.T, reduce_weight])[None])
    bits = [1 << i for i in range(nt.bit_length() - 1)]
    near_in = gather_across(nt, both[:, 0].reshape(-1, full), bits)
    near_out = gather_across(nt, both[:, 1].reshape(-1, full).T, bits[::-1])
    halves_in = [jnp.stack([near_in[s] for s in range(nt)])]
    halves_in.append(flip(halves_in[0], "seq", ns, 1))
    halves_out = [jnp.stack([near_out[s] for s in range(nt)])]
    halves_out.append(flip(halves_out[0], "seq", ns, 1))

    def exchange(x):
        return lax.all_to_all(x, "seq", split_axis=0, concat_axis=0, tiled=True)

    def first(at, n, deps=()):
        return first_pass(at, n, activations, first_factor, spectral, ns, deps)

    def second(front, m, deps=(), groups=1):
        return second_pass(front, m, second_factor, groups, deps)

    def gated(k, back, deps=(), group=0):
        return gate(k, group, me, activations, back, scale, shift, nt, list(deps))

    def layer(slots, deps=()):
        return mlp(me, slots, halves_in, halves_out, list(deps))

    def put(k, done, result, group=0):
        return place(k, group, me, done, result, activations.shape)

    front01 = exchange(after(first(0, 2), got[0], got[2]))
    front23 = exchange(after(first(1, 2), got[1]))
    (mixed0,) = second(front01, 0, [near_in[bits[0]], near_out[bits[-1]]])
    (mixed1,) = second(front01, 1)
    back0 = exchange(mixed0)
    (mixed2,) = second(front23, 0, [halves_in[0], halves_out[0]])
    back1 = exchange(mixed1)
    (mixed3,) = second(front23, 1, [halves_in[1], halves_out[1]])
    in0 = swap(gated(0, back0))
    back2 = exchange(after(mixed2, *in0[1:]))
    gate1 = gated(1, back1)
    in1 = swap(gate1)
    out0 = layer(in0, [gate1[0]])
    back3 = exchange(after(mixed3, out0[0], *in1[1:]))
    done0 = swap(out0)
    gate2 = gated(2, back2)
    in2 = swap(gate2)
    out1 = layer(in1, [gate2[0]])
    done1 = swap(out1)
    result = put(0, done0, None)
    gate3 = gated(3, back3, [out1[0], in2[1]])
    in3 = swap(gate3)
    out2 = layer(in2, [gate3[0], result])
    done2 = swap(out2)
    result = put(1, done1, result)
    out3 = layer(in3, [out2[0]])
    done3 = swap(out3)
    result = put(2, done2, result)
    return put(3, done3, result)


def solution(mesh):
    return jax.shard_map(
        functools.partial(on_device, mesh.shape["seq"], mesh.shape["tensor"]),
        mesh=mesh,
        in_specs=(
            P("tensor", "seq"),
            P(),
            P("tensor", "seq"),
            P(),
            P(),
            P(),
            P(None, ("seq", "tensor")),
            P(("seq", "tensor"), None),
        ),
        out_specs=P("tensor", "seq"),
        check_vma=False,
    )
```

```python
import functools

import jax
import jax.numpy as jnp
from jax import lax
from jax.experimental import pallas as pl
from jax.experimental.pallas import tpu as pltpu
from jax.sharding import PartitionSpec as P

B = 512
J = 128
epsilon = 1e-06
f32 = jnp.float32
bf16 = jnp.bfloat16
ANY = pl.BlockSpec(memory_space=pl.ANY)


def params(mib):
    return pltpu.CompilerParams(vmem_limit_bytes=mib * 2**20)


def first_pass(at, n, activations, first_factor, spectral, ns, deps=()):
    c, tokens = activations.shape
    blocks = tokens // B
    step = min(4, blocks)
    wide = n * J
    per = B // wide

    def kernel(act, factor, *rest):
        specs, out = rest[:step], rest[-1]
        for q in range(step):
            product = jnp.dot(act[:, q * B : (q + 1) * B], factor[...], preferred_element_type=f32)
            value = (product * specs[q][...]).astype(bf16)
            for m in range(n):
                out[:, m, q] = value[:, m * J : (m + 1) * J].reshape(ns, c // ns, J)

    def spec_at(q):
        return pl.BlockSpec((c, wide), lambda i: (0, (i * step + q) * per + at))

    return pl.pallas_call(
        kernel,
        grid=(blocks // step,),
        in_specs=[
            pl.BlockSpec((c, step * B), lambda i: (0, i)),
            pl.BlockSpec((B, wide), lambda i: (0, at)),
        ]
        + [spec_at(q) for q in range(step)]
        + [ANY] * len(deps),
        out_specs=pl.BlockSpec((ns, n, step, c // ns, J), lambda i: (0, 0, i, 0, 0)),
        out_shape=jax.ShapeDtypeStruct((ns, n, blocks, c // ns, J), bf16),
        compiler_params=params(32),
        cost_estimate=pl.CostEstimate(
            flops=2 * c * blocks * B * wide,
            bytes_accessed=2 * c * tokens + 6 * c * blocks * wide,
            transcendentals=0,
        ),
    )(activations, first_factor, *[spectral] * step, *deps)


def second_pass(gathered, m, second_factor, groups, deps=()):
    ns, _, blocks, c, _ = gathered.shape
    a = ns * blocks
    cb = min(16, c)
    part = blocks // groups

    def kernel(x_ref, s_ref, *rest):
        outs, (x_wide, y_wide) = rest[-groups - 2 : -2], rest[-2:]
        x_wide[...] = x_ref[...].astype(f32).reshape(a * cb, J)
        factor = s_ref[...]
        high = factor.astype(bf16)
        low = (factor - high.astype(f32)).astype(bf16)
        for i in range(0, cb, 2):
            x = jnp.concatenate(
                [x_wide[pl.ds(i + h, a, stride=cb), :] for h in range(2)], axis=1
            ).astype(bf16)
            y = jnp.dot(high, x, preferred_element_type=f32)
            y += jnp.dot(low, x, preferred_element_type=f32)
            for h in range(2):
                y_wide[pl.ds(i + h, a, stride=cb), :] = y[:, h * J : (h + 1) * J]
        y = y_wide[...].reshape(ns, blocks, cb, J)
        for g in range(groups):
            outs[g][...] = y[:, g * part : (g + 1) * part].astype(bf16)

    return pl.pallas_call(
        kernel,
        grid=(c // cb,),
        in_specs=[
            pl.BlockSpec((ns, 1, blocks, cb, J), lambda i: (0, m, 0, i, 0)),
            pl.BlockSpec((a, a), lambda i: (0, 0)),
        ]
        + [ANY] * len(deps),
        out_specs=[pl.BlockSpec((ns, part, cb, J), lambda i: (0, 0, i, 0))] * groups,
        out_shape=[jax.ShapeDtypeStruct((ns, part, c, J), bf16)] * groups,
        scratch_shapes=[pltpu.VMEM((a * cb, J), f32), pltpu.VMEM((a * cb, J), f32)],
        compiler_params=params(32),
        cost_estimate=pl.CostEstimate(
            flops=8 * a * a * c * J, bytes_accessed=4 * a * c * J, transcendentals=0
        ),
    )(gathered, second_factor, *deps)


def gate(k, group, me, activations, returned, scale, shift, nt, deps):
    c, tokens = activations.shape
    ns, blocks, ci, _ = returned.shape
    mine = blocks // nt
    step = min(2, mine)
    steps = mine // step
    begin = group * blocks // step

    def kernel(me_ref, *rest):
        acts, rets = rest[:nt], rest[nt : 2 * nt]
        scale_ref, shift_ref = rest[2 * nt : 2 * nt + 2]
        outs = rest[-nt:]
        for s in range(nt):
            for q in range(step):
                x = acts[s][:, q * B + k * J : q * B + (k + 1) * J].astype(f32)
                mixed = rets[s][:, q].reshape(c, J).astype(f32)
                gating = jax.nn.sigmoid(x * scale_ref[...] + shift_ref[...])
                outs[s][:, q * J : (q + 1) * J] = (x + gating * mixed).astype(bf16)

    def act_at(s):
        return pl.BlockSpec((c, step * B), lambda i, me: (0, begin + (me[0] ^ s) * steps + i))

    def ret_at(s):
        return pl.BlockSpec(
            (ns, step, ci, J), lambda i, me: (0, (me[0] ^ s) * steps + i, 0, 0)
        )

    column = pl.BlockSpec((c, 1), lambda i, me: (0, 0))
    return pl.pallas_call(
        kernel,
        grid_spec=pltpu.PrefetchScalarGridSpec(
            num_scalar_prefetch=1,
            grid=(steps,),
            in_specs=[act_at(s) for s in range(nt)]
            + [ret_at(s) for s in range(nt)]
            + [column, column]
            + [ANY] * len(deps),
            out_specs=[pl.BlockSpec((c, step * J), lambda i, me: (0, i))] * nt,
        ),
        out_shape=[jax.ShapeDtypeStruct((c, mine * J), bf16)] * nt,
        compiler_params=params(56),
        cost_estimate=pl.CostEstimate(
            flops=8 * c * blocks * J,
            bytes_accessed=2 * c * tokens + 4 * c * blocks * J,
            transcendentals=c * blocks * J,
        ),
    )(me, *[activations] * nt, *[returned] * nt, scale, shift, *deps)


def mlp(me, slots, halves_in, halves_out, deps):
    nt = len(slots)
    c, tokens = slots[0].shape
    half, hb, full = halves_in[0].shape
    n = 2 * half
    tile = min(256, tokens)

    def kernel(me_ref, *rest):
        xs, w1s, w2s = rest[:nt], rest[nt : nt + 2], rest[nt + 2 : nt + 4]
        outs = rest[-nt - 5 : -5]
        normed, total, w1, w2, sems = rest[-5:]
        step = pl.program_id(0)

        def fetch(piece, slot):
            return (
                pltpu.make_async_copy(
                    w1s[piece // half].at[piece % half], w1.at[slot], sems.at[0, slot]
                ),
                pltpu.make_async_copy(
                    w2s[piece // half].at[piece % half], w2.at[slot], sems.at[1, slot]
                ),
            )

        def start(piece):
            for copy in fetch(piece, piece % 2):
                copy.start()

        @pl.when(step == 0)
        def _():
            start(0)
            squares = jnp.zeros((1, tokens), f32)
            for s in range(nt):
                x = xs[s][...].astype(f32)
                squares += jnp.sum(x * x, axis=0, keepdims=True)
            scale = lax.rsqrt(squares / full + epsilon)
            for s in range(nt):
                at = pl.multiple_of((me_ref[0] ^ s) * c, c)
                normed[pl.ds(at, c), :] = (xs[s][...].astype(f32) * scale).astype(bf16)
            total[...] = jnp.zeros_like(total)

        for piece in range(1, n):
            pl.when(step == piece - 1)(functools.partial(start, piece))
        slot = lax.rem(step, 2)
        for copy in fetch(0, slot):
            copy.wait()

        def expand(t):
            return jnp.dot(w1[slot], normed[:, t : t + tile], preferred_element_type=f32)

        ahead = expand(0)
        for t in range(0, tokens, tile):
            x = ahead
            if t + tile < tokens:
                ahead = expand(t + tile)
            h = jax.nn.gelu(x).astype(bf16)
            total[:, t : t + tile] += jnp.dot(w2[slot], h, preferred_element_type=f32)

        @pl.when(step == n - 1)
        def _():
            for s in range(nt):
                at = pl.multiple_of((me_ref[0] ^ s) * c, c)
                outs[s][...] = (xs[s][...].astype(f32) + total[pl.ds(at, c), :]).astype(bf16)

    whole = pl.BlockSpec((c, tokens), lambda i, me: (0, 0))
    return pl.pallas_call(
        kernel,
        grid_spec=pltpu.PrefetchScalarGridSpec(
            num_scalar_prefetch=1,
            grid=(n,),
            in_specs=[whole] * nt + [ANY] * (4 + len(deps)),
            out_specs=[whole] * nt,
            scratch_shapes=[
                pltpu.VMEM((full, tokens), bf16),
                pltpu.VMEM((full, tokens), f32),
                pltpu.VMEM((2, hb, full), bf16),
                pltpu.VMEM((2, full, hb), bf16),
                pltpu.SemaphoreType.DMA((2, 2)),
            ],
        ),
        out_shape=[jax.ShapeDtypeStruct((c, tokens), bf16)] * nt,
        compiler_params=params(40),
        cost_estimate=pl.CostEstimate(
            flops=4 * full * hb * n * tokens,
            bytes_accessed=4 * full * hb * n + 4 * full * tokens,
            transcendentals=hb * n * tokens,
        ),
    )(me, *slots, *halves_in, *halves_out, *deps)


def place(k, group, me, slots, result, shape):
    nt = len(slots)
    c, tokens = slots[0].shape
    mine = tokens // J
    given = [] if result is None else [result]

    def kernel(me_ref, *rest):
        ys, out, sems = rest[:nt], rest[-2], rest[-1]
        copies = []
        for s in range(nt):
            for q in range(mine):
                block = group * nt * mine + (me_ref[0] ^ s) * mine + q
                at = pl.multiple_of(block * B + k * J, J)
                copies.append(
                    pltpu.make_async_copy(
                        ys[s].at[:, q * J : (q + 1) * J],
                        out.at[:, pl.ds(at, J)],
                        sems.at[s * mine + q],
                    )
                )
        for copy in copies:
            copy.start()
        for copy in copies:
            copy.wait()

    return pl.pallas_call(
        kernel,
        in_specs=[pl.BlockSpec(memory_space=pltpu.SMEM)]
        + [pl.BlockSpec(memory_space=pltpu.VMEM)] * nt
        + [ANY] * len(given),
        out_specs=ANY,
        out_shape=jax.ShapeDtypeStruct(shape, bf16),
        scratch_shapes=[pltpu.SemaphoreType.DMA((nt * mine,))],
        compiler_params=params(16),
        input_output_aliases={1 + nt: 0} if given else {},
        cost_estimate=pl.CostEstimate(
            flops=0, bytes_accessed=4 * c * tokens * nt, transcendentals=0
        ),
    )(me, *slots, *given)


def swap(slots):
    n = len(slots)
    return [slots[0]] + [
        lax.ppermute(slots[s], "tensor", [(i, i ^ s) for i in range(n)]) for s in range(1, n)
    ]


def after(x, *deps):
    return pl.pallas_call(
        lambda *refs: None,
        in_specs=[ANY] * (1 + len(deps)),
        out_specs=ANY,
        out_shape=jax.ShapeDtypeStruct(x.shape, x.dtype),
        input_output_aliases={0: 0},
    )(x, *deps)


def flip(x, axis, n, bit):
    return lax.ppermute(x, axis, [(i, i ^ bit) for i in range(n)])


def gather_along(ns, both):
    got = [flip(both, "seq", ns, 2)]
    both = jnp.concatenate([both, got[0]])
    bit = 4
    if ns % 8 == 0:
        middle = [i for i in range(ns) if ((i >> 1) ^ (i >> 2)) & 1]
        got.append(lax.ppermute(both, "seq", [(i, i ^ 6) for i in middle]))
        got.append(lax.ppermute(got[1], "seq", [(i, i ^ 2) for i in middle]))
        both = jnp.concatenate([both, got[1] + got[2]])
        bit = 8
    while bit < ns:
        got.append(flip(both, "seq", ns, bit))
        both = jnp.concatenate([both, got[-1]])
        bit *= 2
    return both, got


def gather_across(nt, start, order):
    pieces = {0: start}
    for bit in order:
        pieces |= {s ^ bit: flip(x, "tensor", nt, bit) for s, x in pieces.items()}
    return pieces


def on_device(
    ns,
    nt,
    activations,
    first_factor,
    spectral,
    second_factor,
    gate_scale,
    gate_shift,
    expand_weight,
    reduce_weight,
):
    c = activations.shape[0]
    full = reduce_weight.shape[1]
    at = lax.axis_index("tensor")
    me = at.astype(jnp.int32).reshape(1)
    scale = lax.dynamic_slice_in_dim(gate_scale, at * c, c)[:, None]
    shift = lax.dynamic_slice_in_dim(gate_shift, at * c, c)[:, None]
    both, got = gather_along(ns, jnp.stack([expand_weight.T, reduce_weight])[None])
    bits = [1 << i for i in range(nt.bit_length() - 1)]
    near_in = gather_across(nt, both[:, 0].reshape(-1, full), bits)
    near_out = gather_across(nt, both[:, 1].reshape(-1, full).T, bits[::-1])
    halves_in = [jnp.stack([near_in[s] for s in range(nt)])]
    halves_in.append(flip(halves_in[0], "seq", ns, 1))
    halves_out = [jnp.stack([near_out[s] for s in range(nt)])]
    halves_out.append(flip(halves_out[0], "seq", ns, 1))

    def exchange(x):
        return lax.all_to_all(x, "seq", split_axis=0, concat_axis=0, tiled=True)

    def first(at, n, deps=()):
        return first_pass(at, n, activations, first_factor, spectral, ns, deps)

    def second(front, m, deps=(), groups=1):
        return second_pass(front, m, second_factor, groups, deps)

    def gated(k, back, deps=(), group=0):
        return gate(k, group, me, activations, back, scale, shift, nt, list(deps))

    def layer(slots, deps=()):
        return mlp(me, slots, halves_in, halves_out, list(deps))

    def put(k, done, result, group=0):
        return place(k, group, me, done, result, activations.shape)

    front01 = exchange(after(first(0, 2), got[1]))
    front23 = exchange(after(first(1, 2), got[-1]))
    (mixed0,) = second(front01, 0, [near_in[bits[0]], near_out[bits[-1]]])
    (mixed1,) = second(front01, 1)
    back0 = exchange(mixed0)
    (mixed2,) = second(front23, 0, [halves_in[0], halves_out[0]])
    back1 = exchange(mixed1)
    (mixed3,) = second(front23, 1, [halves_in[1], halves_out[1]])
    in0 = swap(gated(0, back0))
    back2 = exchange(after(mixed2, *in0[1:]))
    gate1 = gated(1, back1)
    in1 = swap(gate1)
    out0 = layer(in0, [gate1[0]])
    back3 = exchange(after(mixed3, out0[0], *in1[1:]))
    done0 = swap(out0)
    gate2 = gated(2, back2)
    in2 = swap(gate2)
    out1 = layer(in1, [gate2[0]])
    done1 = swap(out1)
    result = put(0, done0, None)
    gate3 = gated(3, back3, [out1[0], in2[1], result])
    in3 = swap(gate3)
    out2 = layer(in2, [gate3[0]])
    done2 = swap(out2)
    out3 = layer(in3, [out2[0], *done1[1:3]])
    done3 = swap(out3)
    result = put(1, done1, result)
    result = put(2, done2, result)
    return put(3, done3, result)


def solution(mesh):
    return jax.shard_map(
        functools.partial(on_device, mesh.shape["seq"], mesh.shape["tensor"]),
        mesh=mesh,
        in_specs=(
            P("tensor", "seq"),
            P(),
            P("tensor", "seq"),
            P(),
            P(),
            P(),
            P(None, ("seq", "tensor")),
            P(("seq", "tensor"), None),
        ),
        out_specs=P("tensor", "seq"),
        check_vma=False,
    )
```

```python
import functools

import jax
import jax.numpy as jnp
from jax import lax
from jax.experimental import pallas as pl
from jax.experimental.pallas import tpu as pltpu
from jax.sharding import PartitionSpec as P

B = 512
J = 128
epsilon = 1e-06
f32 = jnp.float32
bf16 = jnp.bfloat16
ANY = pl.BlockSpec(memory_space=pl.ANY)


def params(mib):
    return pltpu.CompilerParams(vmem_limit_bytes=mib * 2**20)


def first_pass(at, n, activations, first_factor, spectral, ns, deps=()):
    c, tokens = activations.shape
    blocks = tokens // B
    step = min(4, blocks)
    wide = n * J
    per = B // wide

    def kernel(act, factor, *rest):
        specs, out = rest[:step], rest[-1]
        for q in range(step):
            product = jnp.dot(act[:, q * B : (q + 1) * B], factor[...], preferred_element_type=f32)
            value = (product * specs[q][...]).astype(bf16)
            for m in range(n):
                out[:, m, q] = value[:, m * J : (m + 1) * J].reshape(ns, c // ns, J)

    def spec_at(q):
        return pl.BlockSpec((c, wide), lambda i: (0, (i * step + q) * per + at))

    return pl.pallas_call(
        kernel,
        grid=(blocks // step,),
        in_specs=[
            pl.BlockSpec((c, step * B), lambda i: (0, i)),
            pl.BlockSpec((B, wide), lambda i: (0, at)),
        ]
        + [spec_at(q) for q in range(step)]
        + [ANY] * len(deps),
        out_specs=pl.BlockSpec((ns, n, step, c // ns, J), lambda i: (0, 0, i, 0, 0)),
        out_shape=jax.ShapeDtypeStruct((ns, n, blocks, c // ns, J), bf16),
        compiler_params=params(32),
        cost_estimate=pl.CostEstimate(
            flops=2 * c * blocks * B * wide,
            bytes_accessed=2 * c * tokens + 6 * c * blocks * wide,
            transcendentals=0,
        ),
    )(activations, first_factor, *[spectral] * step, *deps)


def second_pass(gathered, m, second_factor, groups, deps=()):
    ns, _, blocks, c, _ = gathered.shape
    a = ns * blocks
    cb = min(16, c)
    part = blocks // groups

    def kernel(x_ref, s_ref, *rest):
        outs, (x_wide, y_wide) = rest[-groups - 2 : -2], rest[-2:]
        x_wide[...] = x_ref[...].astype(f32).reshape(a * cb, J)
        factor = s_ref[...]
        high = factor.astype(bf16)
        low = (factor - high.astype(f32)).astype(bf16)
        for i in range(0, cb, 2):
            x = jnp.concatenate(
                [x_wide[pl.ds(i + h, a, stride=cb), :] for h in range(2)], axis=1
            ).astype(bf16)
            y = jnp.dot(high, x, preferred_element_type=f32)
            y += jnp.dot(low, x, preferred_element_type=f32)
            for h in range(2):
                y_wide[pl.ds(i + h, a, stride=cb), :] = y[:, h * J : (h + 1) * J]
        y = y_wide[...].reshape(ns, blocks, cb, J)
        for g in range(groups):
            outs[g][...] = y[:, g * part : (g + 1) * part].astype(bf16)

    return pl.pallas_call(
        kernel,
        grid=(c // cb,),
        in_specs=[
            pl.BlockSpec((ns, 1, blocks, cb, J), lambda i: (0, m, 0, i, 0)),
            pl.BlockSpec((a, a), lambda i: (0, 0)),
        ]
        + [ANY] * len(deps),
        out_specs=[pl.BlockSpec((ns, part, cb, J), lambda i: (0, 0, i, 0))] * groups,
        out_shape=[jax.ShapeDtypeStruct((ns, part, c, J), bf16)] * groups,
        scratch_shapes=[pltpu.VMEM((a * cb, J), f32), pltpu.VMEM((a * cb, J), f32)],
        compiler_params=params(32),
        cost_estimate=pl.CostEstimate(
            flops=8 * a * a * c * J, bytes_accessed=4 * a * c * J, transcendentals=0
        ),
    )(gathered, second_factor, *deps)


def gate(k, group, me, activations, returned, scale, shift, nt, deps):
    c, tokens = activations.shape
    ns, blocks, ci, _ = returned.shape
    mine = blocks // nt
    step = min(2, mine)
    steps = mine // step
    begin = group * blocks // step

    def kernel(me_ref, *rest):
        acts, rets = rest[:nt], rest[nt : 2 * nt]
        scale_ref, shift_ref = rest[2 * nt : 2 * nt + 2]
        outs = rest[-nt:]
        for s in range(nt):
            for q in range(step):
                x = acts[s][:, q * B + k * J : q * B + (k + 1) * J].astype(f32)
                mixed = rets[s][:, q].reshape(c, J).astype(f32)
                gating = jax.nn.sigmoid(x * scale_ref[...] + shift_ref[...])
                outs[s][:, q * J : (q + 1) * J] = (x + gating * mixed).astype(bf16)

    def act_at(s):
        return pl.BlockSpec((c, step * B), lambda i, me: (0, begin + (me[0] ^ s) * steps + i))

    def ret_at(s):
        return pl.BlockSpec(
            (ns, step, ci, J), lambda i, me: (0, (me[0] ^ s) * steps + i, 0, 0)
        )

    column = pl.BlockSpec((c, 1), lambda i, me: (0, 0))
    return pl.pallas_call(
        kernel,
        grid_spec=pltpu.PrefetchScalarGridSpec(
            num_scalar_prefetch=1,
            grid=(steps,),
            in_specs=[act_at(s) for s in range(nt)]
            + [ret_at(s) for s in range(nt)]
            + [column, column]
            + [ANY] * len(deps),
            out_specs=[pl.BlockSpec((c, step * J), lambda i, me: (0, i))] * nt,
        ),
        out_shape=[jax.ShapeDtypeStruct((c, mine * J), bf16)] * nt,
        compiler_params=params(56),
        cost_estimate=pl.CostEstimate(
            flops=8 * c * blocks * J,
            bytes_accessed=2 * c * tokens + 4 * c * blocks * J,
            transcendentals=c * blocks * J,
        ),
    )(me, *[activations] * nt, *[returned] * nt, scale, shift, *deps)


def mlp(me, slots, halves_in, halves_out, deps):
    nt = len(slots)
    c, tokens = slots[0].shape
    half, hb, full = halves_in[0].shape
    n = 2 * half
    tile = min(256, tokens)

    def kernel(me_ref, *rest):
        xs, w1s, w2s = rest[:nt], rest[nt : nt + 2], rest[nt + 2 : nt + 4]
        outs = rest[-nt - 5 : -5]
        normed, total, w1, w2, sems = rest[-5:]
        step = pl.program_id(0)

        def fetch(piece, slot):
            return (
                pltpu.make_async_copy(
                    w1s[piece // half].at[piece % half], w1.at[slot], sems.at[0, slot]
                ),
                pltpu.make_async_copy(
                    w2s[piece // half].at[piece % half], w2.at[slot], sems.at[1, slot]
                ),
            )

        def start(piece):
            for copy in fetch(piece, piece % 2):
                copy.start()

        @pl.when(step == 0)
        def _():
            start(0)
            squares = jnp.zeros((1, tokens), f32)
            for s in range(nt):
                x = xs[s][...].astype(f32)
                squares += jnp.sum(x * x, axis=0, keepdims=True)
            scale = lax.rsqrt(squares / full + epsilon)
            for s in range(nt):
                at = pl.multiple_of((me_ref[0] ^ s) * c, c)
                normed[pl.ds(at, c), :] = (xs[s][...].astype(f32) * scale).astype(bf16)
            total[...] = jnp.zeros_like(total)

        for piece in range(1, n):
            pl.when(step == piece - 1)(functools.partial(start, piece))
        slot = lax.rem(step, 2)
        for copy in fetch(0, slot):
            copy.wait()

        def expand(t):
            return jnp.dot(w1[slot], normed[:, t : t + tile], preferred_element_type=f32)

        ahead = expand(0)
        for t in range(0, tokens, tile):
            x = ahead
            if t + tile < tokens:
                ahead = expand(t + tile)
            h = jax.nn.gelu(x).astype(bf16)
            total[:, t : t + tile] += jnp.dot(w2[slot], h, preferred_element_type=f32)

        @pl.when(step == n - 1)
        def _():
            for s in range(nt):
                at = pl.multiple_of((me_ref[0] ^ s) * c, c)
                outs[s][...] = (xs[s][...].astype(f32) + total[pl.ds(at, c), :]).astype(bf16)

    whole = pl.BlockSpec((c, tokens), lambda i, me: (0, 0))
    return pl.pallas_call(
        kernel,
        grid_spec=pltpu.PrefetchScalarGridSpec(
            num_scalar_prefetch=1,
            grid=(n,),
            in_specs=[whole] * nt + [ANY] * (4 + len(deps)),
            out_specs=[whole] * nt,
            scratch_shapes=[
                pltpu.VMEM((full, tokens), bf16),
                pltpu.VMEM((full, tokens), f32),
                pltpu.VMEM((2, hb, full), bf16),
                pltpu.VMEM((2, full, hb), bf16),
                pltpu.SemaphoreType.DMA((2, 2)),
            ],
        ),
        out_shape=[jax.ShapeDtypeStruct((c, tokens), bf16)] * nt,
        compiler_params=params(40),
        cost_estimate=pl.CostEstimate(
            flops=4 * full * hb * n * tokens,
            bytes_accessed=4 * full * hb * n + 4 * full * tokens,
            transcendentals=hb * n * tokens,
        ),
    )(me, *slots, *halves_in, *halves_out, *deps)


def place(k, group, me, slots, result, shape):
    nt = len(slots)
    c, tokens = slots[0].shape
    mine = tokens // J
    given = [] if result is None else [result]

    def kernel(me_ref, *rest):
        ys, out, sems = rest[:nt], rest[-2], rest[-1]
        copies = []
        for s in range(nt):
            for q in range(mine):
                block = group * nt * mine + (me_ref[0] ^ s) * mine + q
                at = pl.multiple_of(block * B + k * J, J)
                copies.append(
                    pltpu.make_async_copy(
                        ys[s].at[:, q * J : (q + 1) * J],
                        out.at[:, pl.ds(at, J)],
                        sems.at[s * mine + q],
                    )
                )
        for copy in copies:
            copy.start()
        for copy in copies:
            copy.wait()

    return pl.pallas_call(
        kernel,
        in_specs=[pl.BlockSpec(memory_space=pltpu.SMEM)]
        + [pl.BlockSpec(memory_space=pltpu.VMEM)] * nt
        + [ANY] * len(given),
        out_specs=ANY,
        out_shape=jax.ShapeDtypeStruct(shape, bf16),
        scratch_shapes=[pltpu.SemaphoreType.DMA((nt * mine,))],
        compiler_params=params(16),
        input_output_aliases={1 + nt: 0} if given else {},
        cost_estimate=pl.CostEstimate(
            flops=0, bytes_accessed=4 * c * tokens * nt, transcendentals=0
        ),
    )(me, *slots, *given)


def swap(slots):
    n = len(slots)
    return [slots[0]] + [
        lax.ppermute(slots[s], "tensor", [(i, i ^ s) for i in range(n)]) for s in range(1, n)
    ]


def after(x, *deps):
    return pl.pallas_call(
        lambda *refs: None,
        in_specs=[ANY] * (1 + len(deps)),
        out_specs=ANY,
        out_shape=jax.ShapeDtypeStruct(x.shape, x.dtype),
        input_output_aliases={0: 0},
    )(x, *deps)


def flip(x, axis, n, bit):
    return lax.ppermute(x, axis, [(i, i ^ bit) for i in range(n)])


def gather_along(ns, both):
    got = [flip(both, "seq", ns, 2)]
    both = jnp.concatenate([both, got[0]])
    bit = 4
    if ns % 8 == 0:
        middle = [i for i in range(ns) if ((i >> 1) ^ (i >> 2)) & 1]
        got.append(lax.ppermute(both, "seq", [(i, i ^ 6) for i in middle]))
        got.append(lax.ppermute(got[1], "seq", [(i, i ^ 2) for i in middle]))
        both = jnp.concatenate([both, got[1] + got[2]])
        bit = 8
    while bit < ns:
        got.append(flip(both, "seq", ns, bit))
        both = jnp.concatenate([both, got[-1]])
        bit *= 2
    return both, got


def gather_across(nt, start, order):
    pieces = {0: start}
    for bit in order:
        pieces |= {s ^ bit: flip(x, "tensor", nt, bit) for s, x in pieces.items()}
    return pieces


def on_device(
    ns,
    nt,
    activations,
    first_factor,
    spectral,
    second_factor,
    gate_scale,
    gate_shift,
    expand_weight,
    reduce_weight,
):
    c = activations.shape[0]
    full = reduce_weight.shape[1]
    at = lax.axis_index("tensor")
    me = at.astype(jnp.int32).reshape(1)
    scale = lax.dynamic_slice_in_dim(gate_scale, at * c, c)[:, None]
    shift = lax.dynamic_slice_in_dim(gate_shift, at * c, c)[:, None]
    both, got = gather_along(ns, jnp.stack([expand_weight.T, reduce_weight])[None])
    bits = [1 << i for i in range(nt.bit_length() - 1)]
    near_in = gather_across(nt, both[:, 0].reshape(-1, full), bits)
    near_out = gather_across(nt, both[:, 1].reshape(-1, full).T, bits[::-1])
    halves_in = [jnp.stack([near_in[s] for s in range(nt)])]
    halves_in.append(flip(halves_in[0], "seq", ns, 1))
    halves_out = [jnp.stack([near_out[s] for s in range(nt)])]
    halves_out.append(flip(halves_out[0], "seq", ns, 1))

    def exchange(x):
        return lax.all_to_all(x, "seq", split_axis=0, concat_axis=0, tiled=True)

    def first(at, n, deps=()):
        return first_pass(at, n, activations, first_factor, spectral, ns, deps)

    def second(front, m, deps=(), groups=1):
        return second_pass(front, m, second_factor, groups, deps)

    def gated(k, back, deps=(), group=0):
        return gate(k, group, me, activations, back, scale, shift, nt, list(deps))

    def layer(slots, deps=()):
        return mlp(me, slots, halves_in, halves_out, list(deps))

    def put(k, done, result, group=0):
        return place(k, group, me, done, result, activations.shape)

    front01 = exchange(after(first(0, 2), got[1]))
    front23 = exchange(after(first(1, 2), got[-1]))
    (mixed0,) = second(front01, 0, [near_in[bits[0]], near_out[bits[-1]]])
    (mixed1,) = second(front01, 1)
    back0 = exchange(mixed0)
    (mixed2,) = second(front23, 0, [halves_in[0], halves_out[0]])
    back1 = exchange(mixed1)
    (mixed3,) = second(front23, 1, [halves_in[1], halves_out[1]])
    in0 = swap(gated(0, back0))
    back2 = exchange(after(mixed2, *in0[1:]))
    gate1 = gated(1, back1)
    in1 = swap(gate1)
    out0 = layer(in0, [gate1[0]])
    back3 = exchange(after(mixed3, out0[0], *in1[1:]))
    done0 = swap(out0)
    gate2 = gated(2, back2)
    in2 = swap(gate2)
    out1 = layer(in1, [gate2[0]])
    done1 = swap(out1)
    result = put(0, [after(done0[0], out1[0]), *done0[1:]], None)
    gate3 = gated(3, back3, [out1[0], in2[1], result])
    in3 = swap(gate3)
    out2 = layer(in2, [gate3[0]])
    done2 = swap(out2)
    out3 = layer(in3, [out2[0], *done1[1:3]])
    done3 = swap(out3)
    result = put(1, done1, result)
    result = put(2, done2, result)
    return put(3, done3, result)


def solution(mesh):
    return jax.shard_map(
        functools.partial(on_device, mesh.shape["seq"], mesh.shape["tensor"]),
        mesh=mesh,
        in_specs=(
            P("tensor", "seq"),
            P(),
            P("tensor", "seq"),
            P(),
            P(),
            P(),
            P(None, ("seq", "tensor")),
            P(("seq", "tensor"), None),
        ),
        out_specs=P("tensor", "seq"),
        check_vma=False,
    )
```

```python
import functools

import jax
import jax.numpy as jnp
from jax import lax
from jax.experimental import pallas as pl
from jax.experimental.pallas import tpu as pltpu
from jax.sharding import PartitionSpec as P

B = 512
J = 128
epsilon = 1e-06
f32 = jnp.float32
bf16 = jnp.bfloat16
ANY = pl.BlockSpec(memory_space=pl.ANY)


def params(mib):
    return pltpu.CompilerParams(vmem_limit_bytes=mib * 2**20)


def first_pass(at, n, activations, first_factor, spectral, ns, deps=()):
    c, tokens = activations.shape
    blocks = tokens // B
    step = min(4, blocks)
    wide = n * J
    per = B // wide

    def kernel(act, factor, *rest):
        specs, out = rest[:step], rest[-1]
        for q in range(step):
            product = jnp.dot(act[:, q * B : (q + 1) * B], factor[...], preferred_element_type=f32)
            value = (product * specs[q][...]).astype(bf16)
            for m in range(n):
                out[:, m, q] = value[:, m * J : (m + 1) * J].reshape(ns, c // ns, J)

    def spec_at(q):
        return pl.BlockSpec((c, wide), lambda i: (0, (i * step + q) * per + at))

    return pl.pallas_call(
        kernel,
        grid=(blocks // step,),
        in_specs=[
            pl.BlockSpec((c, step * B), lambda i: (0, i)),
            pl.BlockSpec((B, wide), lambda i: (0, at)),
        ]
        + [spec_at(q) for q in range(step)]
        + [ANY] * len(deps),
        out_specs=pl.BlockSpec((ns, n, step, c // ns, J), lambda i: (0, 0, i, 0, 0)),
        out_shape=jax.ShapeDtypeStruct((ns, n, blocks, c // ns, J), bf16),
        compiler_params=params(32),
        cost_estimate=pl.CostEstimate(
            flops=2 * c * blocks * B * wide,
            bytes_accessed=2 * c * tokens + 6 * c * blocks * wide,
            transcendentals=0,
        ),
    )(activations, first_factor, *[spectral] * step, *deps)


def second_pass(gathered, m, second_factor, groups, deps=()):
    ns, _, blocks, c, _ = gathered.shape
    a = ns * blocks
    cb = min(16, c)
    part = blocks // groups

    def kernel(x_ref, s_ref, *rest):
        outs, (x_wide, y_wide) = rest[-groups - 2 : -2], rest[-2:]
        x_wide[...] = x_ref[...].astype(f32).reshape(a * cb, J)
        factor = s_ref[...]
        high = factor.astype(bf16)
        low = (factor - high.astype(f32)).astype(bf16)
        for i in range(0, cb, 2):
            x = jnp.concatenate(
                [x_wide[pl.ds(i + h, a, stride=cb), :] for h in range(2)], axis=1
            ).astype(bf16)
            y = jnp.dot(high, x, preferred_element_type=f32)
            y += jnp.dot(low, x, preferred_element_type=f32)
            for h in range(2):
                y_wide[pl.ds(i + h, a, stride=cb), :] = y[:, h * J : (h + 1) * J]
        y = y_wide[...].reshape(ns, blocks, cb, J)
        for g in range(groups):
            outs[g][...] = y[:, g * part : (g + 1) * part].astype(bf16)

    return pl.pallas_call(
        kernel,
        grid=(c // cb,),
        in_specs=[
            pl.BlockSpec((ns, 1, blocks, cb, J), lambda i: (0, m, 0, i, 0)),
            pl.BlockSpec((a, a), lambda i: (0, 0)),
        ]
        + [ANY] * len(deps),
        out_specs=[pl.BlockSpec((ns, part, cb, J), lambda i: (0, 0, i, 0))] * groups,
        out_shape=[jax.ShapeDtypeStruct((ns, part, c, J), bf16)] * groups,
        scratch_shapes=[pltpu.VMEM((a * cb, J), f32), pltpu.VMEM((a * cb, J), f32)],
        compiler_params=params(32),
        cost_estimate=pl.CostEstimate(
            flops=8 * a * a * c * J, bytes_accessed=4 * a * c * J, transcendentals=0
        ),
    )(gathered, second_factor, *deps)


def gate(k, group, me, activations, returned, scale, shift, nt, deps):
    c, tokens = activations.shape
    ns, blocks, ci, _ = returned.shape
    mine = blocks // nt
    step = min(2, mine)
    steps = mine // step
    begin = group * blocks // step

    def kernel(me_ref, *rest):
        acts, rets = rest[:nt], rest[nt : 2 * nt]
        scale_ref, shift_ref = rest[2 * nt : 2 * nt + 2]
        outs = rest[-nt:]
        for s in range(nt):
            for q in range(step):
                x = acts[s][:, q * B + k * J : q * B + (k + 1) * J].astype(f32)
                mixed = rets[s][:, q].reshape(c, J).astype(f32)
                gating = jax.nn.sigmoid(x * scale_ref[...] + shift_ref[...])
                outs[s][:, q * J : (q + 1) * J] = (x + gating * mixed).astype(bf16)

    def act_at(s):
        return pl.BlockSpec((c, step * B), lambda i, me: (0, begin + (me[0] ^ s) * steps + i))

    def ret_at(s):
        return pl.BlockSpec(
            (ns, step, ci, J), lambda i, me: (0, (me[0] ^ s) * steps + i, 0, 0)
        )

    column = pl.BlockSpec((c, 1), lambda i, me: (0, 0))
    return pl.pallas_call(
        kernel,
        grid_spec=pltpu.PrefetchScalarGridSpec(
            num_scalar_prefetch=1,
            grid=(steps,),
            in_specs=[act_at(s) for s in range(nt)]
            + [ret_at(s) for s in range(nt)]
            + [column, column]
            + [ANY] * len(deps),
            out_specs=[pl.BlockSpec((c, step * J), lambda i, me: (0, i))] * nt,
        ),
        out_shape=[jax.ShapeDtypeStruct((c, mine * J), bf16)] * nt,
        compiler_params=params(56),
        cost_estimate=pl.CostEstimate(
            flops=8 * c * blocks * J,
            bytes_accessed=2 * c * tokens + 4 * c * blocks * J,
            transcendentals=c * blocks * J,
        ),
    )(me, *[activations] * nt, *[returned] * nt, scale, shift, *deps)


def mlp(me, slots, halves_in, halves_out, deps):
    nt = len(slots)
    c, tokens = slots[0].shape
    half, hb, full = halves_in[0].shape
    n = 2 * half
    tile = min(512, tokens)

    def kernel(me_ref, *rest):
        xs, w1s, w2s = rest[:nt], rest[nt : nt + 2], rest[nt + 2 : nt + 4]
        outs = rest[-nt - 5 : -5]
        normed, total, w1, w2, sems = rest[-5:]
        step = pl.program_id(0)

        def fetch(piece, slot):
            return (
                pltpu.make_async_copy(
                    w1s[piece // half].at[piece % half], w1.at[slot], sems.at[0, slot]
                ),
                pltpu.make_async_copy(
                    w2s[piece // half].at[piece % half], w2.at[slot], sems.at[1, slot]
                ),
            )

        def start(piece):
            for copy in fetch(piece, piece % 2):
                copy.start()

        @pl.when(step == 0)
        def _():
            start(0)
            squares = jnp.zeros((1, tokens), f32)
            for s in range(nt):
                x = xs[s][...].astype(f32)
                squares += jnp.sum(x * x, axis=0, keepdims=True)
            scale = lax.rsqrt(squares / full + epsilon)
            for s in range(nt):
                at = pl.multiple_of((me_ref[0] ^ s) * c, c)
                normed[pl.ds(at, c), :] = (xs[s][...].astype(f32) * scale).astype(bf16)
            total[...] = jnp.zeros_like(total)

        for piece in range(1, n):
            pl.when(step == piece - 1)(functools.partial(start, piece))
        slot = lax.rem(step, 2)
        for copy in fetch(0, slot):
            copy.wait()

        def expand(t):
            return jnp.dot(w1[slot], normed[:, t : t + tile], preferred_element_type=f32)

        ahead = expand(0)
        for t in range(0, tokens, tile):
            x = ahead
            if t + tile < tokens:
                ahead = expand(t + tile)
            h = jax.nn.gelu(x).astype(bf16)
            total[:, t : t + tile] += jnp.dot(w2[slot], h, preferred_element_type=f32)

        @pl.when(step == n - 1)
        def _():
            for s in range(nt):
                at = pl.multiple_of((me_ref[0] ^ s) * c, c)
                outs[s][...] = (xs[s][...].astype(f32) + total[pl.ds(at, c), :]).astype(bf16)

    whole = pl.BlockSpec((c, tokens), lambda i, me: (0, 0))
    return pl.pallas_call(
        kernel,
        grid_spec=pltpu.PrefetchScalarGridSpec(
            num_scalar_prefetch=1,
            grid=(n,),
            in_specs=[whole] * nt + [ANY] * (4 + len(deps)),
            out_specs=[whole] * nt,
            scratch_shapes=[
                pltpu.VMEM((full, tokens), bf16),
                pltpu.VMEM((full, tokens), f32),
                pltpu.VMEM((2, hb, full), bf16),
                pltpu.VMEM((2, full, hb), bf16),
                pltpu.SemaphoreType.DMA((2, 2)),
            ],
        ),
        out_shape=[jax.ShapeDtypeStruct((c, tokens), bf16)] * nt,
        compiler_params=params(40),
        cost_estimate=pl.CostEstimate(
            flops=4 * full * hb * n * tokens,
            bytes_accessed=4 * full * hb * n + 4 * full * tokens,
            transcendentals=hb * n * tokens,
        ),
    )(me, *slots, *halves_in, *halves_out, *deps)


def place(k, group, me, slots, result, shape):
    nt = len(slots)
    c, tokens = slots[0].shape
    mine = tokens // J
    given = [] if result is None else [result]

    def kernel(me_ref, *rest):
        ys, out, sems = rest[:nt], rest[-2], rest[-1]
        copies = []
        for s in range(nt):
            for q in range(mine):
                block = group * nt * mine + (me_ref[0] ^ s) * mine + q
                at = pl.multiple_of(block * B + k * J, J)
                copies.append(
                    pltpu.make_async_copy(
                        ys[s].at[:, q * J : (q + 1) * J],
                        out.at[:, pl.ds(at, J)],
                        sems.at[s * mine + q],
                    )
                )
        for copy in copies:
            copy.start()
        for copy in copies:
            copy.wait()

    return pl.pallas_call(
        kernel,
        in_specs=[pl.BlockSpec(memory_space=pltpu.SMEM)]
        + [pl.BlockSpec(memory_space=pltpu.VMEM)] * nt
        + [ANY] * len(given),
        out_specs=ANY,
        out_shape=jax.ShapeDtypeStruct(shape, bf16),
        scratch_shapes=[pltpu.SemaphoreType.DMA((nt * mine,))],
        compiler_params=params(16),
        input_output_aliases={1 + nt: 0} if given else {},
        cost_estimate=pl.CostEstimate(
            flops=0, bytes_accessed=4 * c * tokens * nt, transcendentals=0
        ),
    )(me, *slots, *given)


def swap(slots):
    n = len(slots)
    return [slots[0]] + [
        lax.ppermute(slots[s], "tensor", [(i, i ^ s) for i in range(n)]) for s in range(1, n)
    ]


def after(x, *deps):
    return pl.pallas_call(
        lambda *refs: None,
        in_specs=[ANY] * (1 + len(deps)),
        out_specs=ANY,
        out_shape=jax.ShapeDtypeStruct(x.shape, x.dtype),
        input_output_aliases={0: 0},
    )(x, *deps)


def flip(x, axis, n, bit):
    return lax.ppermute(x, axis, [(i, i ^ bit) for i in range(n)])


def gather_along(ns, both):
    got = [flip(both, "seq", ns, 2)]
    both = jnp.concatenate([both, got[0]])
    bit = 4
    if ns % 8 == 0:
        middle = [i for i in range(ns) if ((i >> 1) ^ (i >> 2)) & 1]
        got.append(lax.ppermute(both, "seq", [(i, i ^ 6) for i in middle]))
        got.append(lax.ppermute(got[1], "seq", [(i, i ^ 2) for i in middle]))
        both = jnp.concatenate([both, got[1] + got[2]])
        bit = 8
    while bit < ns:
        got.append(flip(both, "seq", ns, bit))
        both = jnp.concatenate([both, got[-1]])
        bit *= 2
    return both, got


def gather_across(nt, start, order):
    pieces = {0: start}
    for bit in order:
        pieces |= {s ^ bit: flip(x, "tensor", nt, bit) for s, x in pieces.items()}
    return pieces


def on_device(
    ns,
    nt,
    activations,
    first_factor,
    spectral,
    second_factor,
    gate_scale,
    gate_shift,
    expand_weight,
    reduce_weight,
):
    c = activations.shape[0]
    full = reduce_weight.shape[1]
    at = lax.axis_index("tensor")
    me = at.astype(jnp.int32).reshape(1)
    scale = lax.dynamic_slice_in_dim(gate_scale, at * c, c)[:, None]
    shift = lax.dynamic_slice_in_dim(gate_shift, at * c, c)[:, None]
    both, got = gather_along(ns, jnp.stack([expand_weight.T, reduce_weight])[None])
    bits = [1 << i for i in range(nt.bit_length() - 1)]
    near_in = gather_across(nt, both[:, 0].reshape(-1, full), bits)
    near_out = gather_across(nt, both[:, 1].reshape(-1, full).T, bits[::-1])
    halves_in = [jnp.stack([near_in[s] for s in range(nt)])]
    halves_in.append(flip(halves_in[0], "seq", ns, 1))
    halves_out = [jnp.stack([near_out[s] for s in range(nt)])]
    halves_out.append(flip(halves_out[0], "seq", ns, 1))

    def exchange(x):
        return lax.all_to_all(x, "seq", split_axis=0, concat_axis=0, tiled=True)

    def first(at, n, deps=()):
        return first_pass(at, n, activations, first_factor, spectral, ns, deps)

    def second(front, m, deps=(), groups=1):
        return second_pass(front, m, second_factor, groups, deps)

    def gated(k, back, deps=(), group=0):
        return gate(k, group, me, activations, back, scale, shift, nt, list(deps))

    def layer(slots, deps=()):
        return mlp(me, slots, halves_in, halves_out, list(deps))

    def put(k, done, result, group=0):
        return place(k, group, me, done, result, activations.shape)

    front01 = exchange(after(first(0, 2), got[1]))
    front23 = exchange(after(first(1, 2), got[-1]))
    (mixed0,) = second(front01, 0, [near_in[bits[0]], near_out[bits[-1]]])
    (mixed1,) = second(front01, 1)
    back0 = exchange(mixed0)
    (mixed2,) = second(front23, 0, [halves_in[0], halves_out[0]])
    back1 = exchange(mixed1)
    (mixed3,) = second(front23, 1, [halves_in[1], halves_out[1]])
    in0 = swap(gated(0, back0))
    back2 = exchange(after(mixed2, *in0[1:]))
    gate1 = gated(1, back1)
    in1 = swap(gate1)
    out0 = layer(in0, [gate1[0]])
    back3 = exchange(after(mixed3, out0[0], *in1[1:]))
    done0 = swap(out0)
    gate2 = gated(2, back2)
    in2 = swap(gate2)
    out1 = layer(in1, [gate2[0]])
    done1 = swap(out1)
    result = put(0, [after(done0[0], out1[0]), *done0[1:]], None)
    gate3 = gated(3, back3, [out1[0], in2[1], result])
    in3 = swap(gate3)
    out2 = layer(in2, [gate3[0]])
    done2 = swap(out2)
    out3 = layer(in3, [out2[0], *done1[1:3]])
    done3 = swap(out3)
    result = put(1, done1, result)
    result = put(2, done2, result)
    return put(3, done3, result)


def solution(mesh):
    return jax.shard_map(
        functools.partial(on_device, mesh.shape["seq"], mesh.shape["tensor"]),
        mesh=mesh,
        in_specs=(
            P("tensor", "seq"),
            P(),
            P("tensor", "seq"),
            P(),
            P(),
            P(),
            P(None, ("seq", "tensor")),
            P(("seq", "tensor"), None),
        ),
        out_specs=P("tensor", "seq"),
        check_vma=False,
    )
```
